512 devices in a mesh: leaf: 64 (over y, x, core), head: 8 (over z).
Axes of the slice: x: 4, y: 8, z: 8, core: 2. Of those that a mesh axis runs over, the one named last changes fastest.
Arguments:
- queries: bfloat16 [16384, 6144], P('leaf', 'head'), may hold values from -6 to 6
- key_rows: bfloat16 [16384, 1024], P(('leaf', 'head')), may hold values from -6 to 6
- value_rows: bfloat16 [16384, 1024], P(('leaf', 'head')), may hold values from -6 to 6
- out_grad: bfloat16 [16384, 6144], P('leaf', 'head'), may hold values from -6 to 6
- ancestry: int32 [128, 128], replicated, may hold values from 0 to 1, as said below
- block_fill: int32 [128], replicated, may hold values from 32 to 128, as said below
Outputs:
- attn_out: bfloat16 [16384, 6144], P('leaf', 'head')
- query_grad: bfloat16 [16384, 6144], P('leaf', 'head')
- key_grad: bfloat16 [16384, 1024], P('leaf', 'head')
- value_grad: bfloat16 [16384, 1024], P('leaf', 'head')
The draws below stay inside these ranges and needn't reach their ends.
Inputs may be any that keep to these rules, and one draw needn't show every extreme that they name: ancestry[b, a] is 1 exactly when a = b, a = 0, or block a is an ancestor of block b in the tree of reasoning steps, else 0. Every ancestor a > 0 of b has a < b and a >= (b // 2 - 3) * 2; some block has an ancestor at exactly that limit. block_fill[b] is 128 when block b + 1 continues the step of block b.
All inputs are finite; a program needn't handle non-finite values.
Results may differ from the reference program's by a relative error of at most 0.012.
The reference program's roundings to bfloat16 on the way (of `weights_b` and `d_scores`) count: a program that leaves them out, or rounds other values in their place, can miss the bound.
Values may be sent and summed in bfloat16 or wider, within the bound.
A program may use at most 64 MiB of HBM per device.

```python
import math
import jax
import jax.numpy as jnp
from jax import lax

HEADS = 48
KV_HEADS = 8
HD = 128
BLK = 128
REACH = 4
TOK_DEV = 256
TOKENS = 16384
BLOCKS = 128


def step_tree(key):
    blocks_dev = TOK_DEV // BLK
    longest = (REACH - 1) * blocks_dev + 1
    tree_key = jax.random.fold_in(key, 500)
    key_one, key_two = jax.random.split(tree_key)
    coins = jax.random.randint(key_one, (BLOCKS,), 0, longest, dtype=jnp.int32)
    picks = jax.random.randint(key_two, (BLOCKS,), 0, 1 << 20, dtype=jnp.int32)

    def visit_block(running, blk_idx):
        seg_start, run_length = running
        opens = jnp.where(blk_idx <= longest, blk_idx == 1, (run_length >= longest) | (coins[blk_idx] == 0))
        span_len = jnp.maximum(blk_idx - seg_start, 1)
        parent_now = jnp.where(opens, 0, seg_start + picks[blk_idx] % span_len)
        parent_now = jnp.where(blk_idx == longest, 1, parent_now)
        new_start = jnp.where(opens, blk_idx, seg_start)
        new_length = jnp.where(opens, 1, run_length + 1)
        return ((new_start, new_length), parent_now.astype(jnp.int32))
    begin = (jnp.zeros((), jnp.int32), jnp.zeros((), jnp.int32))
    ignored, parents = lax.scan(visit_block, begin, jnp.arange(1, BLOCKS, dtype=jnp.int32))
    parent = jnp.concatenate([jnp.zeros((1,), jnp.int32), parents])
    block_ids = jnp.arange(BLOCKS, dtype=jnp.int32)
    linked = (block_ids[:, None] == block_ids[None, :]) | (block_ids[None, :] == 0)
    climber = parent
    for level in range(longest):
        linked = linked | (climber[:, None] == block_ids[None, :])
        climber = parent[climber]
    return (parent, linked.astype(jnp.int32))


def draw_ancestry(key, part):
    parent, linked = step_tree(key)
    return linked


def draw_block_fill(key, part):
    parent, linked = step_tree(key)
    key = jax.random.fold_in(key, 3)
    block_ids = jnp.arange(BLOCKS, dtype=jnp.int32)
    next_parent = jnp.concatenate([parent[1:], jnp.full((1,), -1, jnp.int32)])
    continued = next_parent == block_ids
    random_fill = jax.random.randint(key, (BLOCKS,), BLK // 4, BLK + 1, dtype=jnp.int32)
    filled = jnp.where(continued, BLK, random_fill)
    filled = filled.at[BLOCKS - 1].set(BLK // 4)
    return filled.astype(jnp.int32)


def draw_queries(key, part):
    key = jax.random.fold_in(key, 1)
    key_one = jax.random.fold_in(key, 0)
    result = jnp.clip(jax.random.normal(key_one, (TOKENS, HEADS * HD), jnp.float32), -6.0, 6.0)
    return result.astype(jnp.bfloat16)


def draw_key_rows(key, part):
    key = jax.random.fold_in(key, 4)
    result = jnp.clip(jax.random.normal(key, (TOKENS, KV_HEADS * HD), jnp.float32), -6.0, 6.0)
    return result.astype(jnp.bfloat16)


def block_levels(stream_key, shape, cuts, low, largest):
    def one(position, blocks):
        steps = jax.random.uniform(jax.random.fold_in(jax.random.fold_in(stream_key, 6), position), (blocks,), jnp.float32, low / len(cuts), largest / len(cuts))
        return jnp.repeat(jnp.exp(steps), shape[position] // blocks).reshape((-1,) + (1,) * (len(shape) - position - 1))

    level = one(*cuts[0])
    for cut in cuts[1:]:
        level = level * one(*cut)
    return level


def centred(key, shape, spread, reach, cuts=(), kind=jnp.bfloat16):
    values = jax.random.normal(key, shape, jnp.float32) * spread
    if len(cuts) > 0:
        values = block_levels(key, shape, cuts, -0.22, 0.18) * values
    return jnp.clip(values, min=-reach, max=reach).astype(kind)


def setup_inputs(seed: int = 0) -> dict:
    splits = jax.random.split(jax.random.key(seed), 7)
    queries = draw_queries(jax.random.fold_in(splits[6], 71), 0)
    key_rows = draw_key_rows(jax.random.fold_in(splits[6], 71), 0)
    value_rows = centred(splits[2], (TOKENS, KV_HEADS * HD), 1.0, 6.0, ((0, 512),))
    out_grad = centred(splits[3], (TOKENS, HEADS * HD), 1.0, 6.0, ((0, 64), (1, 8)))
    ancestry = draw_ancestry(jax.random.fold_in(splits[6], 71), 0)
    block_fill = draw_block_fill(jax.random.fold_in(splits[6], 71), 0)
    return {"queries": queries, "key_rows": key_rows, "value_rows": value_rows, "out_grad": out_grad, "ancestry": ancestry, "block_fill": block_fill}


neg_fill = -1e+30

def reference(queries, key_rows, value_rows, out_grad, ancestry, block_fill):
    blocks_dev = TOK_DEV // BLK
    per_group = HEADS // KV_HEADS
    inv_scale = 1.0 / math.sqrt(HD)
    wide = BLK + REACH * TOK_DEV
    lead = (REACH - 1) * TOK_DEV
    query_heads = queries.reshape(TOKENS, KV_HEADS, per_group, HD)
    grad_heads = out_grad.reshape(TOKENS, KV_HEADS, per_group, HD)
    key_pad = jnp.pad(key_rows, ((lead, 0), (0, 0))).reshape(-1, KV_HEADS, HD)
    value_pad = jnp.pad(value_rows, ((lead, 0), (0, 0))).reshape(-1, KV_HEADS, HD)
    prompt_key = key_rows[:BLK].reshape(BLK, KV_HEADS, HD)
    prompt_value = value_rows[:BLK].reshape(BLK, KV_HEADS, HD)
    anc_pad = jnp.pad(ancestry, ((0, 0), ((REACH - 1) * blocks_dev, 0)))
    fill_pad = jnp.pad(block_fill, (((REACH - 1) * blocks_dev, 0),))

    def visit_block(grad_pad, blk_idx):
        dev_idx = blk_idx // blocks_dev
        q_blk = lax.dynamic_slice_in_dim(query_heads, blk_idx * BLK, BLK, 0).astype(jnp.float32)
        g_blk = lax.dynamic_slice_in_dim(grad_heads, blk_idx * BLK, BLK, 0).astype(jnp.float32)
        k_win = jnp.concatenate([prompt_key, lax.dynamic_slice_in_dim(key_pad, dev_idx * TOK_DEV, REACH * TOK_DEV, 0)], axis=0).astype(jnp.float32)
        v_win = jnp.concatenate([prompt_value, lax.dynamic_slice_in_dim(value_pad, dev_idx * TOK_DEV, REACH * TOK_DEV, 0)], axis=0).astype(jnp.float32)
        anc_row = lax.dynamic_slice_in_dim(ancestry, blk_idx, 1, 0)[0]
        anc_wrow = lax.dynamic_slice_in_dim(anc_pad, blk_idx, 1, 0)[0]
        anc_win = lax.dynamic_slice_in_dim(anc_wrow, dev_idx * blocks_dev, REACH * blocks_dev, 0)
        col_global = (dev_idx - (REACH - 1)) * blocks_dev + jnp.arange(REACH * blocks_dev, dtype=jnp.int32)
        anc_win = jnp.where(col_global >= 1, anc_win, 0)
        links = jnp.concatenate([anc_row[:1], anc_win])
        fills = jnp.concatenate([block_fill[:1], lax.dynamic_slice_in_dim(fill_pad, dev_idx * blocks_dev, REACH * blocks_dev, 0)])
        key_pos = jnp.arange(wide, dtype=jnp.int32)
        key_valid = (jnp.repeat(links, BLK) == 1) & (key_pos % BLK < jnp.repeat(fills, BLK))
        key_global = jnp.concatenate([jnp.arange(BLK, dtype=jnp.int32), (dev_idx - (REACH - 1)) * TOK_DEV + jnp.arange(REACH * TOK_DEV, dtype=jnp.int32)])
        query_global = blk_idx * BLK + jnp.arange(BLK, dtype=jnp.int32)
        allowed = key_valid[None, :] & (key_global[None, :] <= query_global[:, None])
        scores = jnp.einsum('qgjd,kgd->gjqk', q_blk, k_win) * inv_scale
        scores = jnp.where(allowed, scores, neg_fill)
        row_max = lax.optimization_barrier(jnp.max(scores, axis=-1, keepdims=True))
        log_total = row_max + jnp.log(lax.optimization_barrier(jnp.sum(jnp.exp(scores - row_max), axis=-1, keepdims=True)))
        weights = jnp.exp(scores - log_total)
        weights_b = lax.optimization_barrier(weights.astype(jnp.bfloat16)).astype(jnp.float32)
        attended = jnp.einsum('gjqk,kgd->qgjd', weights_b, v_win)
        d_weights = jnp.einsum('qgjd,kgd->gjqk', g_blk, v_win)
        row_delta = jnp.einsum('qgjd,qgjd->gjq', g_blk, attended)[..., None]
        d_scores = lax.optimization_barrier((weights * (d_weights - row_delta)).astype(jnp.bfloat16)).astype(jnp.float32)
        dq_blk = jnp.einsum('gjqk,kgd->qgjd', d_scores, k_win) * inv_scale
        dk_term = jnp.einsum('gjqk,qgjd->kgd', d_scores, q_blk) * inv_scale
        dv_term = jnp.einsum('gjqk,qgjd->kgd', weights_b, g_blk)
        terms = jnp.stack([dk_term, dv_term])
        head_old = lax.dynamic_slice_in_dim(grad_pad, lead, BLK, 1)
        grad_pad = lax.dynamic_update_slice_in_dim(grad_pad, head_old + terms[:, :BLK], lead, 1)
        win_old = lax.dynamic_slice_in_dim(grad_pad, dev_idx * TOK_DEV, REACH * TOK_DEV, 1)
        grad_pad = lax.dynamic_update_slice_in_dim(grad_pad, win_old + terms[:, BLK:], dev_idx * TOK_DEV, 1)
        return (grad_pad, (attended.astype(jnp.bfloat16), dq_blk.astype(jnp.bfloat16)))
    start_grads = jnp.zeros((2, TOKENS + lead, KV_HEADS, HD), jnp.float32)
    grad_pad, outputs = lax.scan(visit_block, start_grads, jnp.arange(BLOCKS, dtype=jnp.int32))
    attn_out = outputs[0].reshape(TOKENS, HEADS * HD)
    query_grad = outputs[1].reshape(TOKENS, HEADS * HD)
    grads = grad_pad[:, lead:].reshape(2, TOKENS, KV_HEADS * HD)
    return (attn_out, query_grad, grads[0].astype(jnp.bfloat16), grads[1].astype(jnp.bfloat16))
```

```python
import functools
import math

import jax
import jax.numpy as jnp
from jax import lax
from jax.experimental import pallas as pl
from jax.experimental.pallas import tpu as pltpu
from jax.sharding import PartitionSpec as P

HD = 128
BLK = 128
REACH = 4
ROW = 8
MESH = pl.DeviceIdType.MESH
NEG = -1e30
NT = (((1,), (1,)), ((), ()))
NN = (((1,), (0,)), ((), ()))
dot = functools.partial(lax.dot_general, preferred_element_type=jnp.float32)


def kernel(
    leaves, groups, queries, key_rows, value_rows, out_grad, ancestry, block_fill,
    attn_out, query_grad, key_grad, value_grad,
    q, g, kv_in, win, win_t, bias, scores, d_weights, row_max, probs, attn, dq,
    grads, own_grad, prompt_grad, prompt_bf, near, part_y, sum_y, part_x, sum_x, prompt_sum,
    final, anc,
    load_sem, store_sem, a2a_send, a2a_recv, shift_send, shift_recv, root_send, root_recv,
    gather_send, gather_recv, grad_send, grad_recv, ry_send, ry_recv, rx_send, rx_recv, rr_send, rr_recv,
):
    leaf = lax.axis_index("leaf")
    head = lax.axis_index("head")
    tok = q.shape[0]
    heads_here = q.shape[1] // HD
    rows_in = kv_in.shape[1]
    rows_y = leaves // ROW
    piece = BLK // rows_y
    wide = win.shape[1]
    own0 = wide - tok
    y = leaf // ROW
    xc = leaf % ROW
    inv_scale = 1.0 / math.sqrt(HD)
    log_scale = inv_scale * math.log2(math.e)

    base = pl.multiple_of((2 * leaf) // 8 * 8, 8)
    loads = [
        pltpu.make_async_copy(key_rows, kv_in.at[0], load_sem.at[0]),
        pltpu.make_async_copy(value_rows, kv_in.at[1], load_sem.at[1]),
        pltpu.make_async_copy(queries, q, load_sem.at[2]),
        pltpu.make_async_copy(out_grad, g, load_sem.at[3]),
        pltpu.make_async_copy(ancestry.at[pl.ds(base, 8)], anc, load_sem.at[4]),
    ]
    for load in loads:
        load.start()

    barrier = pltpu.get_barrier_semaphore()

    def greet(leaf_to, head_to):
        pl.semaphore_signal(barrier, inc=1, device_id=(leaf_to, head_to), device_id_type=MESH)

    for off in range(1, groups):
        greet(leaf, lax.rem(head + off, groups))
    for off in range(1, rows_y):
        greet(lax.rem(y + off, rows_y) * ROW + xc, head)
    for off in range(1, REACH):
        pl.when(leaf >= off)(functools.partial(greet, leaf - off, head))
        pl.when(leaf + off < leaves)(functools.partial(greet, leaf + off, head))

    @pl.when(leaf > 0)
    def _():
        greet(0, head)

    @pl.when(xc == 0)
    def _():
        for off in range(1, ROW):
            greet(leaf + off, head)

    for load in loads[:2]:
        load.wait()
    greeted = groups - 1 + rows_y - 1 + jnp.minimum(leaf, REACH - 1) + jnp.minimum(leaves - 1 - leaf, REACH - 1)
    greeted += jnp.where(xc > 0, 1, 0) + jnp.where(leaf == 0, leaves - 1, 0)
    pl.semaphore_wait(barrier, greeted)

    def remote(src, dst, send, recv, leaf_to, head_to):
        return pltpu.make_async_remote_copy(
            src_ref=src, dst_ref=dst, send_sem=send, recv_sem=recv,
            device_id=(leaf_to, head_to), device_id_type=MESH,
        )

    def a2a_copy(off):
        to = lax.rem(head + off, groups)
        return remote(
            kv_in.at[:, :, pl.ds(pl.multiple_of(to * HD, HD), HD)],
            win.at[:, pl.ds(pl.multiple_of(own0 + head * rows_in, 32), rows_in), :],
            a2a_send.at[off], a2a_recv.at[off], leaf, to,
        )

    for off in range(1, groups):
        a2a_copy(off).start()
    win[:, pl.ds(pl.multiple_of(own0 + head * rows_in, 32), rows_in), :] = kv_in[
        :, :, pl.ds(pl.multiple_of(head * HD, HD), HD)
    ]
    for off in range(1, REACH):
        rows = pl.ds(own0 - off * tok, tok)

        @pl.when(leaf < off)
        def _():
            win[:, rows, :] = jnp.zeros((2, tok, HD), win.dtype)

    loads[4].wait()
    key_iota = lax.broadcasted_iota(jnp.int32, (BLK, BLK), 0)
    query_iota = lax.broadcasted_iota(jnp.int32, (BLK, BLK), 1)
    blocks_dev = tok // BLK
    for col in range(wide // BLK):
        block = 0 if col == 0 else (leaf - (REACH - 1)) * blocks_dev + col - 1
        at = 0 if col == 0 else jnp.maximum(block, 0)
        fill = block_fill[at]
        for row in range(blocks_dev):
            link = anc[2 * leaf - base + row, at]
            if col > 0:
                link = jnp.where(block >= 1, link, 0)
            limit = jnp.where(link == 1, fill, 0)
            allowed = (key_iota < limit) & (
                key_iota + block * BLK <= query_iota + (leaf * blocks_dev + row) * BLK
            )
            bias[col * BLK : (col + 1) * BLK, row * BLK : (row + 1) * BLK] = jnp.where(allowed, 0.0, NEG)
    row_max[...] = jnp.full_like(row_max, NEG)

    for off in range(1, groups):
        a2a_copy(off).wait_recv()

    def shift_copy(off):
        return remote(
            win.at[:, pl.ds(own0, tok), :], win.at[:, pl.ds(own0 - off * tok, tok), :],
            shift_send.at[off], shift_recv.at[off], leaf + off, head,
        )

    def root_copy(to):
        at = to // ROW * piece
        return remote(
            win.at[:, pl.ds(pl.multiple_of(own0 + at, piece), piece), :],
            win.at[:, pl.ds(pl.multiple_of(at, piece), piece), :],
            root_send.at[to], root_recv, to, head,
        )

    @pl.when(leaf == 0)
    def _():
        @pl.loop(1, leaves)
        def _(to):
            root_copy(to).start()

        win[:, :piece, :] = win[:, own0 : own0 + piece, :]

    for off in range(1, REACH):
        pl.when(leaf + off < leaves)(lambda off=off: shift_copy(off).start())

    loads[2].wait()
    loads[3].wait()

    def meet(first, count):
        rows = slice(first, first + count)
        keys, values, added = win[0, rows], win[1, rows], bias[rows]
        for j in range(heads_here):
            cols = slice(j * HD, (j + 1) * HD)
            part = dot(keys, q[:, cols], NT) + added
            scores[j, rows] = part
            row_max[j] = jnp.maximum(row_max[j], part.reshape(count // 8, 8, tok).max(0))
            d_weights[j, rows] = dot(values, g[:, cols], NT)

    meet(own0, tok)

    my_piece = pl.ds(pl.multiple_of(y * piece, piece), piece)

    def gather_copy(off):
        return remote(
            win.at[:, my_piece, :], win.at[:, my_piece, :],
            gather_send.at[off], gather_recv.at[off], lax.rem(y + off, rows_y) * ROW + xc, head,
        )

    @pl.when(leaf > 0)
    def _():
        root_copy(leaf).wait_recv()

    for off in range(1, rows_y):
        gather_copy(off).start()

    for off in range(1, REACH):
        pl.when(leaf >= off)(lambda off=off: shift_copy(off).wait_recv())
        meet(own0 - off * tok, tok)
    for off in range(1, rows_y):
        gather_copy(off).wait_recv()
    meet(0, BLK)
    win_t[0] = win[0].T
    win_t[1] = win[1].T

    step = BLK
    for j in range(heads_here):
        cols = slice(j * HD, (j + 1) * HD)
        top = jnp.max(row_max[j], axis=0, keepdims=True) * log_scale
        total = jnp.zeros((8, tok), jnp.float32)
        delta = jnp.zeros((8, tok), jnp.float32)
        for r in range(0, wide, step):
            rows = slice(r, r + step)
            e = jnp.exp2(scores[j, rows] * log_scale - top)
            scores[j, rows] = e
            total += e.reshape(step // 8, 8, tok).sum(0)
            delta += (e * d_weights[j, rows]).reshape(step // 8, 8, tok).sum(0)
        inverse = 1.0 / total.sum(0, keepdims=True)
        delta = delta.sum(0, keepdims=True) * inverse
        for r in range(0, wide, step):
            rows = slice(r, r + step)
            w = scores[j, rows] * inverse
            probs[0, j, rows] = w.astype(jnp.bfloat16)
            probs[1, j, rows] = (w * (d_weights[j, rows] - delta)).astype(jnp.bfloat16)
        attn[:, cols] = dot(win_t[1], probs[0, j], NN).T.astype(jnp.bfloat16)
    out_copy = pltpu.make_async_copy(attn, attn_out, store_sem.at[0])
    out_copy.start()

    def grad_of(first, count):
        dk = jnp.zeros((count, HD), jnp.float32)
        dv = jnp.zeros((count, HD), jnp.float32)
        for j in range(heads_here):
            cols = slice(j * HD, (j + 1) * HD)
            dk += dot(probs[1, j, first : first + count], q[:, cols], NN)
            dv += dot(probs[0, j, first : first + count], g[:, cols], NN)
        return dk * inv_scale, dv

    def ry_copy(off):
        to = lax.rem(y + off, rows_y)
        return remote(
            prompt_bf.at[:, pl.ds(pl.multiple_of(to * piece, piece), piece), :], part_y.at[off],
            ry_send.at[off], ry_recv.at[off], to * ROW + xc, head,
        )

    dk, dv = grad_of(0, BLK)
    prompt_grad[0], prompt_grad[1] = dk, dv
    prompt_bf[0], prompt_bf[1] = dk.astype(jnp.bfloat16), dv.astype(jnp.bfloat16)
    for off in range(1, rows_y):
        ry_copy(off).start()

    def grad_copy(off):
        return remote(
            grads.at[off], near.at[off], grad_send.at[off], grad_recv.at[off], leaf - off, head
        )

    for off in range(REACH - 1, 0, -1):
        dk, dv = grad_of(own0 - off * tok, tok)
        grads[off, 0], grads[off, 1] = dk.astype(jnp.bfloat16), dv.astype(jnp.bfloat16)
        pl.when(leaf >= off)(lambda off=off: grad_copy(off).start())

    for off in range(1, rows_y):
        ry_copy(off).wait_recv()
    sum_y[...] = prompt_grad[:, my_piece, :]
    for off in range(1, rows_y):
        sum_y[...] += part_y[off].astype(jnp.float32)

    def rx_copy(slot):
        return remote(sum_x.at[0], part_x.at[slot], rx_send, rx_recv.at[slot], y * ROW, head)

    sum_x[0] = sum_y[...].astype(jnp.bfloat16)

    @pl.when(xc > 0)
    def _():
        rx_copy(xc).start()

    own_grad[0], own_grad[1] = grad_of(own0, tok)

    def rr_copy():
        return remote(sum_x.at[1], prompt_sum.at[:, my_piece, :], rr_send, rr_recv.at[y], 0, head)

    @pl.when(xc == 0)
    def _():
        for slot in range(1, ROW):
            rx_copy(slot).wait_recv()
            sum_y[...] += part_x[slot].astype(jnp.float32)

        @pl.when(y > 0)
        def _():
            sum_x[1] = sum_y[...].astype(jnp.bfloat16)
            rr_copy().start()

    for j in range(heads_here):
        cols = slice(j * HD, (j + 1) * HD)
        dq[:, cols] = (dot(win_t[0], probs[1, j], NN).T * inv_scale).astype(jnp.bfloat16)
    dq_copy = pltpu.make_async_copy(dq, query_grad, store_sem.at[1])
    dq_copy.start()

    for off in range(1, REACH):
        @pl.when(leaf + off < leaves)
        def _():
            grad_copy(off).wait_recv()
            own_grad[...] += near[off].astype(jnp.float32)

    @pl.when(leaf == 0)
    def _():
        own_grad[:, :piece, :] += sum_y[...]
        for other in range(1, rows_y):
            rows = slice(other * piece, (other + 1) * piece)
            remote(
                sum_x.at[1], prompt_sum.at[:, rows, :], rr_send, rr_recv.at[other], 0, head
            ).wait_recv()
            own_grad[:, rows, :] += prompt_sum[:, rows, :].astype(jnp.float32)

    final[...] = own_grad[...].astype(jnp.bfloat16)
    last = [
        pltpu.make_async_copy(final.at[0], key_grad, store_sem.at[2]),
        pltpu.make_async_copy(final.at[1], value_grad, store_sem.at[3]),
    ]
    for copy in last:
        copy.start()

    for off in range(1, groups):
        a2a_copy(off).wait_send()
    for off in range(1, REACH):
        pl.when(leaf + off < leaves)(lambda off=off: shift_copy(off).wait_send())
        pl.when(leaf >= off)(lambda off=off: grad_copy(off).wait_send())
    for off in range(1, rows_y):
        gather_copy(off).wait_send()
        ry_copy(off).wait_send()

    @pl.when(leaf == 0)
    def _():
        @pl.loop(1, leaves)
        def _(to):
            root_copy(to).wait_send()

    @pl.when(xc > 0)
    def _():
        rx_copy(xc).wait_send()

    @pl.when((xc == 0) & (y > 0))
    def _():
        rr_copy().wait_send()

    out_copy.wait()
    dq_copy.wait()
    for copy in last:
        copy.wait()


def on_device(leaves, groups, queries, key_rows, value_rows, out_grad, ancestry, block_fill):
    tok, width = queries.shape
    heads_here = width // HD
    wide = BLK + REACH * tok
    piece = BLK // (leaves // ROW)
    bf16, f32 = jnp.bfloat16, jnp.float32
    anywhere = pl.BlockSpec(memory_space=pl.ANY)
    dma = pltpu.SemaphoreType.DMA
    return pl.pallas_call(
        functools.partial(kernel, leaves, groups),
        out_shape=(
            jax.ShapeDtypeStruct((tok, width), bf16),
            jax.ShapeDtypeStruct((tok, width), bf16),
            jax.ShapeDtypeStruct((tok, HD), bf16),
            jax.ShapeDtypeStruct((tok, HD), bf16),
        ),
        in_specs=[anywhere] * 5 + [pl.BlockSpec(memory_space=pltpu.SMEM)],
        out_specs=(anywhere,) * 4,
        scratch_shapes=[
            pltpu.VMEM((tok, width), bf16),
            pltpu.VMEM((tok, width), bf16),
            pltpu.VMEM((2,) + key_rows.shape, bf16),
            pltpu.VMEM((2, wide, HD), bf16),
            pltpu.VMEM((2, HD, wide), bf16),
            pltpu.VMEM((wide, tok), f32),
            pltpu.VMEM((heads_here, wide, tok), f32),
            pltpu.VMEM((heads_here, wide, tok), f32),
            pltpu.VMEM((heads_here, 8, tok), f32),
            pltpu.VMEM((2, heads_here, wide, tok), bf16),
            pltpu.VMEM((tok, width), bf16),
            pltpu.VMEM((tok, width), bf16),
            pltpu.VMEM((REACH, 2, tok, HD), bf16),
            pltpu.VMEM((2, tok, HD), f32),
            pltpu.VMEM((2, BLK, HD), f32),
            pltpu.VMEM((2, BLK, HD), bf16),
            pltpu.VMEM((REACH, 2, tok, HD), bf16),
            pltpu.VMEM((leaves // ROW, 2, piece, HD), bf16),
            pltpu.VMEM((2, piece, HD), f32),
            pltpu.VMEM((ROW, 2, piece, HD), bf16),
            pltpu.VMEM((2, 2, piece, HD), bf16),
            pltpu.VMEM((2, BLK, HD), bf16),
            pltpu.VMEM((2, tok, HD), bf16),
            pltpu.SMEM((8, ancestry.shape[1]), jnp.int32),
            dma((5,)),
            dma((4,)),
            dma((groups,)),
            dma((groups,)),
            dma((REACH,)),
            dma((REACH,)),
            dma((leaves,)),
            dma,
            dma((leaves // ROW,)),
            dma((leaves // ROW,)),
            dma((REACH,)),
            dma((REACH,)),
            dma((leaves // ROW,)),
            dma((leaves // ROW,)),
            dma,
            dma((ROW,)),
            dma,
            dma((leaves // ROW,)),
        ],
        compiler_params=pltpu.CompilerParams(
            collective_id=0, has_side_effects=True, vmem_limit_bytes=50 * 2**20
        ),
    )(queries, key_rows, value_rows, out_grad, ancestry, block_fill)


def solution(mesh):
    placed = (
        P("leaf", "head"),
        P(("leaf", "head"), None),
        P(("leaf", "head"), None),
        P("leaf", "head"),
        P(),
        P(),
    )
    return jax.shard_map(
        functools.partial(on_device, mesh.shape["leaf"], mesh.shape["head"]),
        mesh=mesh,
        in_specs=placed,
        out_specs=(P("leaf", "head"), P("leaf", "head"), P("leaf", "head"), P("leaf", "head")),
        check_vma=False,
    )
```

```python
import functools
import math

import jax
import jax.numpy as jnp
from jax import lax
from jax.experimental import pallas as pl
from jax.experimental.pallas import tpu as pltpu
from jax.sharding import PartitionSpec as P

HD = 128
BLK = 128
REACH = 4
ROW = 8
MESH = pl.DeviceIdType.MESH
NEG = -1e30
NT = (((1,), (1,)), ((), ()))
NN = (((1,), (0,)), ((), ()))
dot = functools.partial(lax.dot_general, preferred_element_type=jnp.float32)


def kernel(
    leaves, groups, queries, key_rows, value_rows, out_grad, ancestry, fills,
    attn_out, query_grad, key_grad, value_grad,
    q, g, kv_in, win, win_t, bias, scores, d_weights, row_max, probs, attn, dq,
    grads, own_grad, prompt_grad, prompt_bf, near, part_x, sum_x, part_root,
    final, anc, block_fill,
    load_sem, store_sem, a2a_send, a2a_recv, shift_send, shift_recv, root_send, root_recv,
    gather_send, gather_recv, grad_send, grad_recv, rx_send, rx_recv, rr_send, rr_recv,
):
    leaf = lax.axis_index("leaf")
    head = lax.axis_index("head")
    tok = q.shape[0]
    heads_here = q.shape[1] // HD
    rows_in = kv_in.shape[1]
    rows_y = leaves // ROW
    piece = BLK // ROW
    wide = win.shape[1]
    own0 = wide - tok
    y = leaf // ROW
    xc = leaf % ROW
    core = leaf % 2
    sibling = leaf + 1 - 2 * core
    inv_scale = 1.0 / math.sqrt(HD)
    log_scale = inv_scale * math.log2(math.e)

    base = pl.multiple_of((2 * leaf) // 8 * 8, 8)
    loads = [
        pltpu.make_async_copy(key_rows, kv_in.at[0], load_sem.at[0]),
        pltpu.make_async_copy(value_rows, kv_in.at[1], load_sem.at[1]),
        pltpu.make_async_copy(queries, q, load_sem.at[2]),
        pltpu.make_async_copy(out_grad, g, load_sem.at[3]),
        pltpu.make_async_copy(ancestry.at[pl.ds(base, 8)], anc, load_sem.at[4]),
        pltpu.make_async_copy(fills, block_fill, load_sem.at[5]),
    ]
    for load in loads:
        load.start()

    pending = []
    barrier = pltpu.get_barrier_semaphore()

    def greet(leaf_to, head_to):
        pl.semaphore_signal(barrier, inc=1, device_id=(leaf_to, head_to), device_id_type=MESH)

    for off in range(1, groups):
        greet(leaf, lax.rem(head + off, groups))
    for off in range(1, ROW):
        greet(y * ROW + lax.rem(xc + off, ROW), head)
    for off in range(1, REACH):
        pl.when(leaf >= off)(functools.partial(greet, leaf - off, head))
        pl.when(leaf + off < leaves)(functools.partial(greet, leaf + off, head))

    @pl.when(leaf > 0)
    def _():
        greet(0, head)

    @pl.when(leaf == 0)
    def _():
        @pl.loop(1, leaves)
        def _(to):
            greet(to, head)

    for load in loads[:2]:
        load.wait()
    greeted = groups - 1 + ROW - 1 + jnp.minimum(leaf, REACH - 1) + jnp.minimum(leaves - 1 - leaf, REACH - 1)
    greeted += jnp.where(leaf == 0, leaves - 1, 1)
    pl.semaphore_wait(barrier, greeted)

    def remote(src, dst, send, recv, leaf_to, head_to):
        return pltpu.make_async_remote_copy(
            src_ref=src, dst_ref=dst, send_sem=send, recv_sem=recv,
            device_id=(leaf_to, head_to), device_id_type=MESH,
        )

    def a2a_copy(off):
        to = lax.rem(head + off, groups)
        return remote(
            kv_in.at[:, :, pl.ds(pl.multiple_of(to * HD, HD), HD)],
            win.at[:, pl.ds(pl.multiple_of(own0 + head * rows_in, 32), rows_in), :],
            a2a_send.at[off], a2a_recv.at[off], leaf, to,
        )

    for off in range(1, groups):
        a2a_copy(off).start()
        pending.append(a2a_copy(off).wait_send)
    win[:, pl.ds(pl.multiple_of(own0 + head * rows_in, 32), rows_in), :] = kv_in[
        :, :, pl.ds(pl.multiple_of(head * HD, HD), HD)
    ]
    for off in range(1, REACH):
        rows = pl.ds(own0 - off * tok, tok)

        @pl.when(leaf < off)
        def _():
            win[:, rows, :] = jnp.zeros((2, tok, HD), win.dtype)

    loads[4].wait()
    loads[5].wait()
    key_iota = lax.broadcasted_iota(jnp.int32, (BLK, BLK), 0)
    query_iota = lax.broadcasted_iota(jnp.int32, (BLK, BLK), 1)
    blocks_dev = tok // BLK
    for col in range(wide // BLK):
        block = 0 if col == 0 else (leaf - (REACH - 1)) * blocks_dev + col - 1
        at = 0 if col == 0 else jnp.maximum(block, 0)
        fill = block_fill[at]
        for row in range(blocks_dev):
            link = anc[2 * leaf - base + row, at]
            if col > 0:
                link = jnp.where(block >= 1, link, 0)
            limit = jnp.where(link == 1, fill, 0)
            allowed = (key_iota < limit) & (
                key_iota + block * BLK <= query_iota + (leaf * blocks_dev + row) * BLK
            )
            bias[col * BLK : (col + 1) * BLK, row * BLK : (row + 1) * BLK] = jnp.where(allowed, 0.0, NEG)
    row_max[...] = jnp.full_like(row_max, NEG)

    for off in range(1, groups):
        a2a_copy(off).wait_recv()

    def chunk(off):
        return pl.ds(pl.multiple_of(own0 - off * tok, BLK), tok)

    side = jnp.where(core == 0, 1, REACH - 1)

    def shift_copy(off):
        return remote(
            win.at[:, pl.ds(own0, tok), :], win.at[:, chunk(off), :],
            shift_send.at[off], shift_recv.at[off], leaf + off, head,
        )

    def swap_copy():
        lands = REACH - side
        return remote(
            win.at[:, chunk(2), :], win.at[:, chunk(lands), :], shift_send.at[0], shift_recv.at[lands], sibling, head
        )

    def root_copy(to):
        at = to % ROW * piece
        return remote(
            win.at[:, pl.ds(pl.multiple_of(own0 + at, piece), piece), :],
            win.at[:, pl.ds(pl.multiple_of(at, piece), piece), :],
            root_send.at[to], root_recv, to, head,
        )

    for off in (2, side):
        @pl.when(leaf + off < leaves)
        def _():
            shift_copy(off).start()

        pending.append(lambda off=off: pl.when(leaf + off < leaves)(lambda: shift_copy(off).wait_send()))

    @pl.when(leaf == 0)
    def _():
        for row in sorted(range(rows_y), key=lambda r: -min(r, rows_y - r)):
            @pl.loop(row * ROW + (row == 0), (row + 1) * ROW)
            def _(to):
                root_copy(to).start()

        win[:, :piece, :] = win[:, own0 : own0 + piece, :]

    def root_done():
        @pl.when(leaf == 0)
        def _():
            @pl.loop(1, leaves)
            def _(to):
                root_copy(to).wait_send()

    pending.append(root_done)

    loads[2].wait()
    loads[3].wait()

    def meet(first, count):
        rows = slice(first, first + count)
        keys, values, added = win[0, rows], win[1, rows], bias[rows]
        for j in range(heads_here):
            cols = slice(j * HD, (j + 1) * HD)
            part = dot(keys, q[:, cols], NT) + added
            scores[j, rows] = part
            row_max[j] = jnp.maximum(row_max[j], part.reshape(count // 8, 8, tok).max(0))
            d_weights[j, rows] = dot(values, g[:, cols], NT)

    meet(own0, tok)

    my_piece = pl.ds(pl.multiple_of(xc * piece, piece), piece)

    def gather_copy(off):
        return remote(
            win.at[:, my_piece, :], win.at[:, my_piece, :],
            gather_send.at[off], gather_recv.at[off], y * ROW + lax.rem(xc + off, ROW), head,
        )

    @pl.when(leaf >= 2)
    def _():
        shift_copy(2).wait_recv()
        swap_copy().start()

    pending.append(lambda: pl.when(leaf >= 2)(lambda: swap_copy().wait_send()))
    meet(own0 - 2 * tok, tok)

    @pl.when(leaf > 0)
    def _():
        root_copy(leaf).wait_recv()

    for off in range(1, ROW):
        gather_copy(off).start()
        pending.append(gather_copy(off).wait_send)
    for off in (1, 3):
        pl.when(leaf >= off)(lambda off=off: shift_copy(off).wait_recv())
        meet(own0 - off * tok, tok)
    for off in range(1, ROW):
        gather_copy(off).wait_recv()
    meet(0, BLK)
    win_t[0] = win[0].T
    win_t[1] = win[1].T

    step = BLK
    for j in range(heads_here):
        cols = slice(j * HD, (j + 1) * HD)
        top = jnp.max(row_max[j], axis=0, keepdims=True) * log_scale
        total = jnp.zeros((8, tok), jnp.float32)
        delta = jnp.zeros((8, tok), jnp.float32)
        for r in range(0, wide, step):
            rows = slice(r, r + step)
            e = jnp.exp2(scores[j, rows] * log_scale - top)
            scores[j, rows] = e
            total += e.reshape(step // 8, 8, tok).sum(0)
            delta += (e * d_weights[j, rows]).reshape(step // 8, 8, tok).sum(0)
        inverse = 1.0 / total.sum(0, keepdims=True)
        delta = delta.sum(0, keepdims=True) * inverse
        for r in range(0, wide, step):
            rows = slice(r, r + step)
            w = scores[j, rows] * inverse
            probs[0, j, rows] = w.astype(jnp.bfloat16)
            probs[1, j, rows] = (w * (d_weights[j, rows] - delta)).astype(jnp.bfloat16)
        attn[:, cols] = dot(win_t[1], probs[0, j], NN).T.astype(jnp.bfloat16)
    out_copy = pltpu.make_async_copy(attn, attn_out, store_sem.at[0])
    out_copy.start()
    pending.append(out_copy.wait)

    def grad_of(rows, count):
        dk = jnp.zeros((count, HD), jnp.float32)
        dv = jnp.zeros((count, HD), jnp.float32)
        for j in range(heads_here):
            cols = slice(j * HD, (j + 1) * HD)
            dk += dot(probs[1, j, rows], q[:, cols], NN)
            dv += dot(probs[0, j, rows], g[:, cols], NN)
        return dk * inv_scale, dv

    def rx_copy(off):
        to = lax.rem(xc + off, ROW)
        return remote(
            prompt_bf.at[:, pl.ds(pl.multiple_of(to * piece, piece), piece), :], part_x.at[off],
            rx_send.at[off], rx_recv.at[off], y * ROW + to, head,
        )

    dk, dv = grad_of(slice(0, BLK), BLK)
    prompt_grad[0], prompt_grad[1] = dk, dv
    prompt_bf[0], prompt_bf[1] = dk.astype(jnp.bfloat16), dv.astype(jnp.bfloat16)
    for off in range(1, ROW):
        rx_copy(off).start()
        pending.append(rx_copy(off).wait_send)

    def grad_copy(slot, to):
        return remote(grads.at[slot], near.at[slot], grad_send.at[slot], grad_recv.at[slot], to, head)

    dk, dv = grad_of(chunk(side), tok)
    grads[0, 0], grads[0, 1] = dk.astype(jnp.bfloat16), dv.astype(jnp.bfloat16)
    pl.when(leaf >= 2)(lambda: grad_copy(0, sibling).start())
    pending.append(lambda: pl.when(leaf >= 2)(lambda: grad_copy(0, sibling).wait_send()))

    own_grad[0], own_grad[1] = grad_of(chunk(2), tok)

    @pl.when(leaf >= 2)
    def _():
        grad_copy(0, sibling).wait_recv()
        grads[1] = (own_grad[...] + near[0].astype(jnp.float32)).astype(jnp.bfloat16)
        grad_copy(1, leaf - 2).start()

    pending.append(lambda: pl.when(leaf >= 2)(lambda: grad_copy(1, leaf - 2).wait_send()))

    rest = REACH - side
    dk, dv = grad_of(chunk(rest), tok)
    grads[2, 0], grads[2, 1] = dk.astype(jnp.bfloat16), dv.astype(jnp.bfloat16)
    pl.when(leaf >= rest)(lambda: grad_copy(2, leaf - rest).start())
    pending.append(lambda: pl.when(leaf >= rest)(lambda: grad_copy(2, leaf - rest).wait_send()))

    def rr_copy():
        return remote(sum_x, part_root.at[leaf], rr_send, rr_recv, 0, head)

    total_x = prompt_grad[:, my_piece, :]
    for off in range(1, ROW):
        rx_copy(off).wait_recv()
        total_x += part_x[off].astype(jnp.float32)
    sum_x[...] = total_x.astype(jnp.bfloat16)

    @pl.when(leaf > 0)
    def _():
        rr_copy().start()

    pending.append(lambda: pl.when(leaf > 0)(lambda: rr_copy().wait_send()))

    own_grad[0], own_grad[1] = grad_of(slice(own0, wide), tok)

    for j in range(heads_here):
        cols = slice(j * HD, (j + 1) * HD)
        dq[:, cols] = (dot(win_t[0], probs[1, j], NN).T * inv_scale).astype(jnp.bfloat16)
    dq_copy = pltpu.make_async_copy(dq, query_grad, store_sem.at[1])
    dq_copy.start()
    pending.append(dq_copy.wait)

    for slot, off in ((1, 2), (2, side)):
        @pl.when(leaf + off < leaves)
        def _():
            grad_copy(slot, leaf).wait_recv()
            own_grad[...] += near[slot].astype(jnp.float32)

    @pl.when(leaf == 0)
    def _():
        others = part_root.at[pl.ds(1, leaves - 1)]
        remote(others, others, rr_send, rr_recv, leaf, head).wait_recv()
        part_root[0] = sum_x[...]
        for slot in range(ROW):
            rows = slice(slot * piece, (slot + 1) * piece)
            for row in range(rows_y):
                own_grad[:, rows, :] += part_root[row * ROW + slot].astype(jnp.float32)

    final[...] = own_grad[...].astype(jnp.bfloat16)
    last = [
        pltpu.make_async_copy(final.at[0], key_grad, store_sem.at[2]),
        pltpu.make_async_copy(final.at[1], value_grad, store_sem.at[3]),
    ]
    for copy in last:
        copy.start()
        pending.append(copy.wait)

    for wait in pending:
        wait()


def store(*refs):
    held, load_sem, store_sem = refs[8:12], refs[12], refs[13]
    loads = [pltpu.make_async_copy(refs[i], held[i], load_sem.at[i]) for i in range(4)]
    stores = [pltpu.make_async_copy(held[i], refs[4 + i], store_sem.at[i]) for i in range(4)]
    for copy in loads:
        copy.start()
    for load, copy in zip(loads, stores):
        load.wait()
        copy.start()
    for copy in stores:
        copy.wait()


def on_device(leaves, groups, queries, key_rows, value_rows, out_grad, ancestry, block_fill):
    tok, width = queries.shape
    heads_here = width // HD
    wide = BLK + REACH * tok
    piece = BLK // ROW
    bf16, f32 = jnp.bfloat16, jnp.float32
    anywhere = pl.BlockSpec(memory_space=pl.ANY)
    in_hbm = pl.BlockSpec(memory_space=pltpu.HBM)
    dma = pltpu.SemaphoreType.DMA
    held = pl.pallas_call(
        functools.partial(kernel, leaves, groups),
        out_shape=(
            jax.ShapeDtypeStruct((tok, width), bf16),
            jax.ShapeDtypeStruct((tok, width), bf16),
            jax.ShapeDtypeStruct((tok, HD), bf16),
            jax.ShapeDtypeStruct((tok, HD), bf16),
        ),
        in_specs=[in_hbm] * 6,
        out_specs=(anywhere,) * 4,
        scratch_shapes=[
            pltpu.VMEM((tok, width), bf16),
            pltpu.VMEM((tok, width), bf16),
            pltpu.VMEM((2,) + key_rows.shape, bf16),
            pltpu.VMEM((2, wide, HD), bf16),
            pltpu.VMEM((2, HD, wide), bf16),
            pltpu.VMEM((wide, tok), f32),
            pltpu.VMEM((heads_here, wide, tok), f32),
            pltpu.VMEM((heads_here, wide, tok), f32),
            pltpu.VMEM((heads_here, 8, tok), f32),
            pltpu.VMEM((2, heads_here, wide, tok), bf16),
            pltpu.VMEM((tok, width), bf16),
            pltpu.VMEM((tok, width), bf16),
            pltpu.VMEM((REACH, 2, tok, HD), bf16),
            pltpu.VMEM((2, tok, HD), f32),
            pltpu.VMEM((2, BLK, HD), f32),
            pltpu.VMEM((2, BLK, HD), bf16),
            pltpu.VMEM((REACH, 2, tok, HD), bf16),
            pltpu.VMEM((ROW, 2, piece, HD), bf16),
            pltpu.VMEM((2, piece, HD), bf16),
            pltpu.VMEM((leaves, 2, piece, HD), bf16),
            pltpu.VMEM((2, tok, HD), bf16),
            pltpu.SMEM((8, ancestry.shape[1]), jnp.int32),
            pltpu.SMEM(block_fill.shape, jnp.int32),
            dma((6,)),
            dma((4,)),
            dma((groups,)),
            dma((groups,)),
            dma((REACH,)),
            dma((REACH,)),
            dma((leaves,)),
            dma,
            dma((ROW,)),
            dma((ROW,)),
            dma((REACH,)),
            dma((REACH,)),
            dma((ROW,)),
            dma((ROW,)),
            dma,
            dma,
        ],
        compiler_params=pltpu.CompilerParams(
            collective_id=0, has_side_effects=True, vmem_limit_bytes=58 * 2**20
        ),
    )(queries, key_rows, value_rows, out_grad, ancestry, block_fill)
    return pl.pallas_call(
        store,
        out_shape=[jax.ShapeDtypeStruct(a.shape, a.dtype) for a in held],
        in_specs=[anywhere] * 4,
        out_specs=[in_hbm] * 4,
        scratch_shapes=[pltpu.VMEM(a.shape, a.dtype) for a in held] + [dma((4,)), dma((4,))],
        compiler_params=pltpu.CompilerParams(vmem_limit_bytes=58 * 2**20),
    )(*held)


def solution(mesh):
    placed = (
        P("leaf", "head"),
        P(("leaf", "head"), None),
        P(("leaf", "head"), None),
        P("leaf", "head"),
        P(),
        P(),
    )
    return jax.shard_map(
        functools.partial(on_device, mesh.shape["leaf"], mesh.shape["head"]),
        mesh=mesh,
        in_specs=placed,
        out_specs=(P("leaf", "head"), P("leaf", "head"), P("leaf", "head"), P("leaf", "head")),
        check_vma=False,
    )
```

```python
import functools
import math

import jax
import jax.numpy as jnp
from jax import lax
from jax.experimental import pallas as pl
from jax.experimental.pallas import tpu as pltpu
from jax.sharding import PartitionSpec as P

HD = 128
BLK = 128
REACH = 4
ROW = 8
MESH = pl.DeviceIdType.MESH
NEG = -1e30
NT = (((1,), (1,)), ((), ()))
NN = (((1,), (0,)), ((), ()))
dot = functools.partial(lax.dot_general, preferred_element_type=jnp.float32)


def kernel(
    leaves, groups, queries, key_rows, value_rows, out_grad, ancestry, fills,
    attn_out, query_grad, key_grad, value_grad,
    q, g, kv_in, win, win_t, bias, scores, d_weights, stats, probs, attn, dq,
    grads, own_grad, prompt_grad, prompt_bf, near, part_x, sum_x, part_root,
    final, anc, block_fill,
    load_sem, store_sem, a2a_send, a2a_recv, shift_send, shift_recv, root_send, root_recv,
    gather_send, gather_recv, grad_send, grad_recv, rx_send, rx_recv, rr_send, rr_recv,
):
    leaf = lax.axis_index("leaf")
    head = lax.axis_index("head")
    tok = q.shape[0]
    heads_here = q.shape[1] // HD
    rows_in = kv_in.shape[1]
    rows_y = leaves // ROW
    piece = BLK // ROW
    wide = win.shape[1]
    own0 = wide - tok
    y = leaf // ROW
    xc = leaf % ROW
    core = leaf % 2
    sibling = leaf + 1 - 2 * core
    inv_scale = 1.0 / math.sqrt(HD)
    log_scale = inv_scale * math.log2(math.e)

    base = pl.multiple_of((2 * leaf) // 8 * 8, 8)
    loads = [
        pltpu.make_async_copy(key_rows, kv_in.at[0], load_sem.at[0]),
        pltpu.make_async_copy(value_rows, kv_in.at[1], load_sem.at[1]),
        pltpu.make_async_copy(queries, q, load_sem.at[2]),
        pltpu.make_async_copy(out_grad, g, load_sem.at[3]),
        pltpu.make_async_copy(ancestry.at[pl.ds(base, 8)], anc, load_sem.at[4]),
        pltpu.make_async_copy(fills, block_fill, load_sem.at[5]),
    ]
    for load in loads:
        load.start()

    pending = []
    barrier = pltpu.get_barrier_semaphore()

    def greet(leaf_to, head_to):
        pl.semaphore_signal(barrier, inc=1, device_id=(leaf_to, head_to), device_id_type=MESH)

    for off in range(1, groups):
        greet(leaf, lax.rem(head + off, groups))
    for off in range(1, ROW):
        greet(y * ROW + lax.rem(xc + off, ROW), head)
    for off in range(1, REACH):
        pl.when(leaf >= off)(functools.partial(greet, leaf - off, head))
        pl.when(leaf + off < leaves)(functools.partial(greet, leaf + off, head))

    @pl.when(leaf > 0)
    def _():
        greet(0, head)

    @pl.when(leaf == 0)
    def _():
        @pl.loop(1, leaves)
        def _(to):
            greet(to, head)

    for load in loads[:2]:
        load.wait()
    greeted = groups - 1 + ROW - 1 + jnp.minimum(leaf, REACH - 1) + jnp.minimum(leaves - 1 - leaf, REACH - 1)
    greeted += jnp.where(leaf == 0, leaves - 1, 1)
    pl.semaphore_wait(barrier, greeted)

    def remote(src, dst, send, recv, leaf_to, head_to):
        return pltpu.make_async_remote_copy(
            src_ref=src, dst_ref=dst, send_sem=send, recv_sem=recv,
            device_id=(leaf_to, head_to), device_id_type=MESH,
        )

    def a2a_copy(off):
        to = lax.rem(head + off, groups)
        return remote(
            kv_in.at[:, :, pl.ds(pl.multiple_of(to * HD, HD), HD)],
            win.at[:, pl.ds(pl.multiple_of(own0 + head * rows_in, 32), rows_in), :],
            a2a_send.at[off], a2a_recv.at[off], leaf, to,
        )

    for off in range(1, groups):
        a2a_copy(off).start()
        pending.append(a2a_copy(off).wait_send)
    win[:, pl.ds(pl.multiple_of(own0 + head * rows_in, 32), rows_in), :] = kv_in[
        :, :, pl.ds(pl.multiple_of(head * HD, HD), HD)
    ]
    for off in range(1, REACH):
        rows = pl.ds(own0 - off * tok, tok)

        @pl.when(leaf < off)
        def _():
            win[:, rows, :] = jnp.zeros((2, tok, HD), win.dtype)

    loads[4].wait()
    loads[5].wait()
    key_iota = lax.broadcasted_iota(jnp.int32, (BLK, BLK), 0)
    query_iota = lax.broadcasted_iota(jnp.int32, (BLK, BLK), 1)
    blocks_dev = tok // BLK
    for col in range(wide // BLK):
        block = 0 if col == 0 else (leaf - (REACH - 1)) * blocks_dev + col - 1
        at = 0 if col == 0 else jnp.maximum(block, 0)
        fill = block_fill[at]
        for row in range(blocks_dev):
            link = anc[2 * leaf - base + row, at]
            if col > 0:
                link = jnp.where(block >= 1, link, 0)
            limit = jnp.where(link == 1, fill, 0)
            allowed = (key_iota < limit) & (
                key_iota + block * BLK <= query_iota + (leaf * blocks_dev + row) * BLK
            )
            bias[col * BLK : (col + 1) * BLK, row * BLK : (row + 1) * BLK] = jnp.where(allowed, 0.0, NEG)

    side = jnp.where(core == 0, 1, REACH - 1)

    parts = max(1, groups // 2)
    part_rows = tok // parts

    def part_of(off, part):
        return win.at[:, pl.ds(pl.multiple_of(own0 - off * tok + part * part_rows, 32), part_rows), :]

    def shift_copy(off, part):
        return remote(
            part_of(0, part), part_of(off, part),
            shift_send.at[off, part], shift_recv.at[off, part], leaf + off, head,
        )

    def swap_copy(part):
        lands = REACH - side
        return remote(
            part_of(2, part), part_of(lands, part),
            shift_send.at[0, part], shift_recv.at[lands, part], sibling, head,
        )

    def root_copy(to):
        at = to % ROW * piece
        return remote(
            win.at[:, pl.ds(pl.multiple_of(own0 + at, piece), piece), :],
            win.at[:, pl.ds(pl.multiple_of(at, piece), piece), :],
            root_send.at[to], root_recv, to, head,
        )

    def scatter():
        for row in sorted(range(rows_y), key=lambda r: -min(r, rows_y - r)):
            @pl.loop(row * ROW + (row == 0), (row + 1) * ROW)
            def _(to):
                root_copy(to).start()

        win[:, :piece, :] = win[:, own0 : own0 + piece, :]

    per_part = groups // parts
    for part in range(parts):
        for source in range(part * per_part, (part + 1) * per_part):
            off = lax.rem(head - source + groups, groups)
            pl.when(off > 0)(lambda off=off: a2a_copy(off).wait_recv())
        if part * part_rows < BLK <= (part + 1) * part_rows:
            pl.when(leaf == 0)(scatter)
        for off in (2, side):
            pl.when(leaf + off < leaves)(lambda off=off: shift_copy(off, part).start())

    def shift_done():
        for part in range(parts):
            for off in (2, side):
                pl.when(leaf + off < leaves)(lambda off=off: shift_copy(off, part).wait_send())

    pending.append(shift_done)

    def root_done():
        @pl.when(leaf == 0)
        def _():
            @pl.loop(1, leaves)
            def _(to):
                root_copy(to).wait_send()

    pending.append(root_done)

    loads[2].wait()
    loads[3].wait()

    def meet(slot, first, count):
        rows = slice(first, first + count)
        keys, values, added = win[0, rows], win[1, rows], bias[rows]
        for j in range(heads_here):
            cols = slice(j * HD, (j + 1) * HD)
            part = dot(keys, q[:, cols], NT) + added
            scores[j, rows] = part
            top = part.reshape(count // 8, 8, tok).max(0).max(0, keepdims=True) * log_scale
            d_weights[j, rows] = dot(values, g[:, cols], NT)
            total = jnp.zeros((8, tok), jnp.float32)
            delta = jnp.zeros((8, tok), jnp.float32)
            for r in range(first, first + count, BLK):
                some = slice(r, r + BLK)
                e = jnp.exp2(scores[j, some] * log_scale - top)
                scores[j, some] = e
                total += e.reshape(BLK // 8, 8, tok).sum(0)
                delta += (e * d_weights[j, some]).reshape(BLK // 8, 8, tok).sum(0)
            stats[slot, j, 0:1] = top
            stats[slot, j, 1:2] = total.sum(0, keepdims=True)
            stats[slot, j, 2:3] = delta.sum(0, keepdims=True)

    meet(1, own0, tok)

    my_piece = pl.ds(pl.multiple_of(xc * piece, piece), piece)

    def gather_copy(off):
        return remote(
            win.at[:, my_piece, :], win.at[:, my_piece, :],
            gather_send.at[off], gather_recv.at[off], y * ROW + lax.rem(xc + off, ROW), head,
        )

    @pl.when(leaf > 0)
    def _():
        root_copy(leaf).wait_recv()

    for off in range(1, ROW):
        gather_copy(off).start()
        pending.append(gather_copy(off).wait_send)

    @pl.when(leaf >= 2)
    def _():
        for part in range(parts):
            shift_copy(2, part).wait_recv()
            swap_copy(part).start()

    def swap_done():
        for part in range(parts):
            swap_copy(part).wait_send()

    pending.append(lambda: pl.when(leaf >= 2)(swap_done))
    meet(3, own0 - 2 * tok, tok)

    for off in (1, 3):
        @pl.when(leaf >= off)
        def _():
            for part in range(parts):
                shift_copy(off, part).wait_recv()

        meet(off + 1, own0 - off * tok, tok)
    for off in range(1, ROW):
        gather_copy(off).wait_recv()
    meet(0, 0, BLK)

    for j in range(heads_here):
        tops = [stats[slot, j, 0:1] for slot in range(REACH + 1)]
        top = functools.reduce(jnp.maximum, tops)
        scales = [jnp.exp2(t - top) for t in tops]
        inverse = 1.0 / sum(stats[slot, j, 1:2] * scales[slot] for slot in range(REACH + 1))
        stats[0, j, 4:5] = inverse * sum(stats[slot, j, 2:3] * scales[slot] for slot in range(REACH + 1))
        for slot in range(REACH + 1):
            stats[slot, j, 3:4] = inverse * scales[slot]

    def grad_of(slot, first, count):
        for j in range(heads_here):
            factor, delta = stats[slot, j, 3:4], stats[0, j, 4:5]
            for r in range(0, count, BLK):
                some = pl.ds(pl.multiple_of(first + r, BLK), BLK)
                w = scores[j, some] * factor
                probs[0, j, some] = w.astype(jnp.bfloat16)
                probs[1, j, some] = (w * (d_weights[j, some] - delta)).astype(jnp.bfloat16)
        rows = pl.ds(pl.multiple_of(first, BLK), count)
        dk = jnp.zeros((count, HD), jnp.float32)
        dv = jnp.zeros((count, HD), jnp.float32)
        for j in range(heads_here):
            cols = slice(j * HD, (j + 1) * HD)
            dk += dot(probs[1, j, rows], q[:, cols], NN)
            dv += dot(probs[0, j, rows], g[:, cols], NN)
        return dk * inv_scale, dv

    def rx_copy(off):
        to = lax.rem(xc + off, ROW)
        return remote(
            prompt_bf.at[:, pl.ds(pl.multiple_of(to * piece, piece), piece), :], part_x.at[off],
            rx_send.at[off], rx_recv.at[off], y * ROW + to, head,
        )

    dk, dv = grad_of(0, 0, BLK)
    prompt_grad[0], prompt_grad[1] = dk, dv
    prompt_bf[0], prompt_bf[1] = dk.astype(jnp.bfloat16), dv.astype(jnp.bfloat16)
    for off in range(1, ROW):
        rx_copy(off).start()
        pending.append(rx_copy(off).wait_send)

    def grad_copy(slot, to):
        return remote(grads.at[slot], near.at[slot], grad_send.at[slot], grad_recv.at[slot], to, head)

    dk, dv = grad_of(side + 1, own0 - side * tok, tok)
    grads[0, 0], grads[0, 1] = dk.astype(jnp.bfloat16), dv.astype(jnp.bfloat16)
    pl.when(leaf >= 2)(lambda: grad_copy(0, sibling).start())
    pending.append(lambda: pl.when(leaf >= 2)(lambda: grad_copy(0, sibling).wait_send()))

    own_grad[0], own_grad[1] = grad_of(3, own0 - 2 * tok, tok)

    @pl.when(leaf >= 2)
    def _():
        grad_copy(0, sibling).wait_recv()
        grads[1] = (own_grad[...] + near[0].astype(jnp.float32)).astype(jnp.bfloat16)
        grad_copy(1, leaf - 2).start()

    pending.append(lambda: pl.when(leaf >= 2)(lambda: grad_copy(1, leaf - 2).wait_send()))

    rest = REACH - side
    dk, dv = grad_of(rest + 1, own0 - rest * tok, tok)
    grads[2, 0], grads[2, 1] = dk.astype(jnp.bfloat16), dv.astype(jnp.bfloat16)
    pl.when(leaf >= rest)(lambda: grad_copy(2, leaf - rest).start())
    pending.append(lambda: pl.when(leaf >= rest)(lambda: grad_copy(2, leaf - rest).wait_send()))

    def rr_copy():
        return remote(sum_x, part_root.at[leaf], rr_send, rr_recv, 0, head)

    total_x = prompt_grad[:, my_piece, :]
    for off in range(1, ROW):
        rx_copy(off).wait_recv()
        total_x += part_x[off].astype(jnp.float32)
    sum_x[...] = total_x.astype(jnp.bfloat16)

    @pl.when(leaf > 0)
    def _():
        rr_copy().start()

    pending.append(lambda: pl.when(leaf > 0)(lambda: rr_copy().wait_send()))

    own_grad[0], own_grad[1] = grad_of(1, own0, tok)

    win_t[0] = win[0].T
    win_t[1] = win[1].T
    for j in range(heads_here):
        cols = slice(j * HD, (j + 1) * HD)
        attn[:, cols] = dot(win_t[1], probs[0, j], NN).T.astype(jnp.bfloat16)
    out_copy = pltpu.make_async_copy(attn, attn_out, store_sem.at[0])
    out_copy.start()
    pending.append(out_copy.wait)
    for j in range(heads_here):
        cols = slice(j * HD, (j + 1) * HD)
        dq[:, cols] = (dot(win_t[0], probs[1, j], NN).T * inv_scale).astype(jnp.bfloat16)
    dq_copy = pltpu.make_async_copy(dq, query_grad, store_sem.at[1])
    dq_copy.start()
    pending.append(dq_copy.wait)

    for slot, off in ((1, 2), (2, side)):
        @pl.when(leaf + off < leaves)
        def _():
            grad_copy(slot, leaf).wait_recv()
            own_grad[...] += near[slot].astype(jnp.float32)

    @pl.when(leaf == 0)
    def _():
        others = part_root.at[pl.ds(1, leaves - 1)]
        remote(others, others, rr_send, rr_recv, leaf, head).wait_recv()
        part_root[0] = sum_x[...]
        for slot in range(ROW):
            rows = slice(slot * piece, (slot + 1) * piece)
            for row in range(rows_y):
                own_grad[:, rows, :] += part_root[row * ROW + slot].astype(jnp.float32)

    final[...] = own_grad[...].astype(jnp.bfloat16)
    last = [
        pltpu.make_async_copy(final.at[0], key_grad, store_sem.at[2]),
        pltpu.make_async_copy(final.at[1], value_grad, store_sem.at[3]),
    ]
    for copy in last:
        copy.start()
        pending.append(copy.wait)

    for wait in pending:
        wait()


def store(*refs):
    copies = [pltpu.make_async_copy(refs[i], refs[4 + i], refs[8].at[i]) for i in range(4)]
    for copy in copies:
        copy.start()
    for copy in copies:
        copy.wait()


def on_device(leaves, groups, queries, key_rows, value_rows, out_grad, ancestry, block_fill):
    tok, width = queries.shape
    heads_here = width // HD
    wide = BLK + REACH * tok
    piece = BLK // ROW
    bf16, f32 = jnp.bfloat16, jnp.float32
    anywhere = pl.BlockSpec(memory_space=pl.ANY)
    in_hbm = pl.BlockSpec(memory_space=pltpu.HBM)
    dma = pltpu.SemaphoreType.DMA
    held = pl.pallas_call(
        functools.partial(kernel, leaves, groups),
        out_shape=(
            pltpu.VMEM((tok, width), bf16),
            pltpu.VMEM((tok, width), bf16),
            pltpu.VMEM((tok, HD), bf16),
            pltpu.VMEM((tok, HD), bf16),
        ),
        in_specs=[in_hbm] * 6,
        out_specs=(anywhere,) * 4,
        scratch_shapes=[
            pltpu.VMEM((tok, width), bf16),
            pltpu.VMEM((tok, width), bf16),
            pltpu.VMEM((2,) + key_rows.shape, bf16),
            pltpu.VMEM((2, wide, HD), bf16),
            pltpu.VMEM((2, HD, wide), bf16),
            pltpu.VMEM((wide, tok), f32),
            pltpu.VMEM((heads_here, wide, tok), f32),
            pltpu.VMEM((heads_here, wide, tok), f32),
            pltpu.VMEM((REACH + 1, heads_here, 8, tok), f32),
            pltpu.VMEM((2, heads_here, wide, tok), bf16),
            pltpu.VMEM((tok, width), bf16),
            pltpu.VMEM((tok, width), bf16),
            pltpu.VMEM((REACH, 2, tok, HD), bf16),
            pltpu.VMEM((2, tok, HD), f32),
            pltpu.VMEM((2, BLK, HD), f32),
            pltpu.VMEM((2, BLK, HD), bf16),
            pltpu.VMEM((REACH, 2, tok, HD), bf16),
            pltpu.VMEM((ROW, 2, piece, HD), bf16),
            pltpu.VMEM((2, piece, HD), bf16),
            pltpu.VMEM((leaves, 2, piece, HD), bf16),
            pltpu.VMEM((2, tok, HD), bf16),
            pltpu.SMEM((8, ancestry.shape[1]), jnp.int32),
            pltpu.SMEM(block_fill.shape, jnp.int32),
            dma((6,)),
            dma((4,)),
            dma((groups,)),
            dma((groups,)),
            dma((REACH, max(1, groups // 2))),
            dma((REACH, max(1, groups // 2))),
            dma((leaves,)),
            dma,
            dma((ROW,)),
            dma((ROW,)),
            dma((REACH,)),
            dma((REACH,)),
            dma((ROW,)),
            dma((ROW,)),
            dma,
            dma,
        ],
        compiler_params=pltpu.CompilerParams(
            collective_id=0, has_side_effects=True, vmem_limit_bytes=50 * 2**20
        ),
    )(
        *(
            pltpu.with_memory_space_constraint(a, pltpu.HBM)
            for a in (queries, key_rows, value_rows, out_grad, ancestry, block_fill)
        )
    )
    return pl.pallas_call(
        store,
        out_shape=[jax.ShapeDtypeStruct(a.shape, a.dtype) for a in held],
        in_specs=[anywhere] * 4,
        out_specs=[in_hbm] * 4,
        scratch_shapes=[dma((4,))],
    )(*(pltpu.with_memory_space_constraint(a, pltpu.VMEM) for a in held))


def solution(mesh):
    placed = (
        P("leaf", "head"),
        P(("leaf", "head"), None),
        P(("leaf", "head"), None),
        P("leaf", "head"),
        P(),
        P(),
    )
    return jax.shard_map(
        functools.partial(on_device, mesh.shape["leaf"], mesh.shape["head"]),
        mesh=mesh,
        in_specs=placed,
        out_specs=(P("leaf", "head"), P("leaf", "head"), P("leaf", "head"), P("leaf", "head")),
        check_vma=False,
    )
```

```python
import functools
import math

import jax
import jax.numpy as jnp
from jax import lax
from jax.experimental import pallas as pl
from jax.experimental.pallas import tpu as pltpu
from jax.sharding import PartitionSpec as P

HD = 128
BLK = 128
REACH = 4
ROW = 8
MESH = pl.DeviceIdType.MESH
NEG = -1e30
NT = (((1,), (1,)), ((), ()))
NN = (((1,), (0,)), ((), ()))
dot = functools.partial(lax.dot_general, preferred_element_type=jnp.float32)


def kernel(
    leaves, groups, queries, key_rows, value_rows, out_grad, ancestry, fills,
    attn_out, query_grad, key_grad, value_grad,
    q, g, kv_in, win, win_t, bias, scores, d_weights, stats, probs, attn, dq,
    grads, own_grad, prompt_grad, prompt_bf, near, part_x, sum_x, part_root,
    final, anc, block_fill,
    load_sem, store_sem, a2a_send, a2a_recv, shift_send, shift_recv, root_send, root_recv,
    gather_send, gather_recv, grad_send, grad_recv, rx_send, rx_recv, rr_send, rr_recv, ready,
):
    leaf = lax.axis_index("leaf")
    head = lax.axis_index("head")
    tok = q.shape[0]
    heads_here = q.shape[1] // HD
    rows_in = kv_in.shape[1]
    rows_y = leaves // ROW
    chips = ROW // 2
    piece = BLK // chips
    wide = win.shape[1]
    own0 = wide - tok
    y = leaf // ROW
    xc = leaf % ROW
    x = xc // 2
    core = leaf % 2
    sibling = leaf + 1 - 2 * core
    inv_scale = 1.0 / math.sqrt(HD)
    log_scale = inv_scale * math.log2(math.e)

    base = pl.multiple_of((2 * leaf) // 8 * 8, 8)
    loads = [
        pltpu.make_async_copy(key_rows, kv_in.at[0], load_sem.at[0]),
        pltpu.make_async_copy(value_rows, kv_in.at[1], load_sem.at[1]),
        pltpu.make_async_copy(queries, q, load_sem.at[2]),
        pltpu.make_async_copy(out_grad, g, load_sem.at[3]),
        pltpu.make_async_copy(ancestry.at[pl.ds(base, 8)], anc, load_sem.at[4]),
        pltpu.make_async_copy(fills, block_fill, load_sem.at[5]),
    ]
    for load in loads[:2]:
        load.start()

    pending = []
    barrier = pltpu.get_barrier_semaphore()

    def greet(leaf_to, head_to):
        pl.semaphore_signal(barrier, inc=1, device_id=(leaf_to, head_to), device_id_type=MESH)

    for off in range(1, groups):
        greet(leaf, lax.rem(head + off, groups))
    for off in range(1, ROW):
        greet(y * ROW + lax.rem(xc + off, ROW), head)
    for off in range(1, REACH):
        pl.when(leaf >= off)(functools.partial(greet, leaf - off, head))
        pl.when(leaf + off < leaves)(functools.partial(greet, leaf + off, head))

    @pl.when(leaf == 0)
    def _():
        @pl.loop(1, leaves)
        def _(to):
            greet(to, head)

    for load in loads[:2]:
        load.wait()
    greeted = groups - 1 + ROW - 1 + jnp.minimum(leaf, REACH - 1) + jnp.minimum(leaves - 1 - leaf, REACH - 1)
    greeted += jnp.where(leaf == 0, 0, 1)
    pl.semaphore_wait(barrier, greeted)

    @pl.when((leaf > 0) & (core == 0))
    def _():
        pl.semaphore_signal(ready, inc=1, device_id=(0, head), device_id_type=MESH)

    def remote(src, dst, send, recv, leaf_to, head_to):
        return pltpu.make_async_remote_copy(
            src_ref=src, dst_ref=dst, send_sem=send, recv_sem=recv,
            device_id=(leaf_to, head_to), device_id_type=MESH,
        )

    def a2a_copy(off):
        to = lax.rem(head + off, groups)
        return remote(
            kv_in.at[:, :, pl.ds(pl.multiple_of(to * HD, HD), HD)],
            win.at[:, pl.ds(pl.multiple_of(own0 + head * rows_in, 32), rows_in), :],
            a2a_send.at[off], a2a_recv.at[off], leaf, to,
        )

    for off in range(1, groups):
        a2a_copy(off).start()
        pending.append(a2a_copy(off).wait_send)
    for load in loads[2:]:
        load.start()
    win[:, pl.ds(pl.multiple_of(own0 + head * rows_in, 32), rows_in), :] = kv_in[
        :, :, pl.ds(pl.multiple_of(head * HD, HD), HD)
    ]
    for off in range(1, REACH):
        rows = pl.ds(own0 - off * tok, tok)

        @pl.when(leaf < off)
        def _():
            win[:, rows, :] = jnp.zeros((2, tok, HD), win.dtype)

    loads[4].wait()
    loads[5].wait()
    key_iota = lax.broadcasted_iota(jnp.int32, (BLK, BLK), 0)
    query_iota = lax.broadcasted_iota(jnp.int32, (BLK, BLK), 1)
    blocks_dev = tok // BLK
    for col in range(wide // BLK):
        block = 0 if col == 0 else (leaf - (REACH - 1)) * blocks_dev + col - 1
        at = 0 if col == 0 else jnp.maximum(block, 0)
        fill = block_fill[at]
        for row in range(blocks_dev):
            link = anc[2 * leaf - base + row, at]
            if col > 0:
                link = jnp.where(block >= 1, link, 0)
            limit = jnp.where(link == 1, fill, 0)
            allowed = (key_iota < limit) & (
                key_iota + block * BLK <= query_iota + (leaf * blocks_dev + row) * BLK
            )
            bias[col * BLK : (col + 1) * BLK, row * BLK : (row + 1) * BLK] = jnp.where(allowed, 0.0, NEG)

    side = jnp.where(core == 0, 1, REACH - 1)

    parts = max(1, groups // 2)
    part_rows = tok // parts

    def part_of(off, part):
        return win.at[:, pl.ds(pl.multiple_of(own0 - off * tok + part * part_rows, 32), part_rows), :]

    def shift_copy(off, part):
        return remote(
            part_of(0, part), part_of(off, part),
            shift_send.at[off, part], shift_recv.at[off, part], leaf + off, head,
        )

    def swap_copy(part):
        lands = REACH - side
        return remote(
            part_of(2, part), part_of(lands, part),
            shift_send.at[0, part], shift_recv.at[lands, part], sibling, head,
        )

    def root_copy(to):
        at = to % ROW // 2 * piece
        return remote(
            win.at[:, pl.ds(pl.multiple_of(own0 + at, piece), piece), :],
            win.at[:, pl.ds(pl.multiple_of(at, piece), piece), :],
            root_send.at[to], root_recv, to, head,
        )

    def scatter():
        pl.semaphore_wait(ready, rows_y * chips - 1)
        for row in sorted(range(rows_y), key=lambda r: -min(r, rows_y - r)):
            @pl.loop(int(row == 0), chips)
            def _(i):
                root_copy(row * ROW + 2 * i).start()

        win[:, :piece, :] = win[:, own0 : own0 + piece, :]

    per_part = groups // parts
    for part in range(parts):
        for source in range(part * per_part, (part + 1) * per_part):
            off = lax.rem(head - source + groups, groups)
            pl.when(off > 0)(lambda off=off: a2a_copy(off).wait_recv())
        for off in (2, side):
            pl.when(leaf + off < leaves)(lambda off=off: shift_copy(off, part).start())
        if part * part_rows < BLK <= (part + 1) * part_rows:
            pl.when(leaf == 0)(scatter)

    def shift_done():
        for part in range(parts):
            for off in (2, side):
                pl.when(leaf + off < leaves)(lambda off=off: shift_copy(off, part).wait_send())

    pending.append(shift_done)

    def root_done():
        @pl.when(leaf == 0)
        def _():
            @pl.loop(1, rows_y * chips)
            def _(i):
                root_copy(2 * i).wait_send()

    pending.append(root_done)

    loads[2].wait()
    loads[3].wait()

    def meet(slot, first, count):
        rows = slice(first, first + count)
        keys, values, added = win[0, rows], win[1, rows], bias[rows]
        for j in range(heads_here):
            cols = slice(j * HD, (j + 1) * HD)
            part = dot(keys, q[:, cols], NT) + added
            scores[j, rows] = part
            top = part.reshape(count // 8, 8, tok).max(0).max(0, keepdims=True) * log_scale
            d_weights[j, rows] = dot(values, g[:, cols], NT)
            total = jnp.zeros((8, tok), jnp.float32)
            delta = jnp.zeros((8, tok), jnp.float32)
            for r in range(first, first + count, BLK):
                some = slice(r, r + BLK)
                e = jnp.exp2(scores[j, some] * log_scale - top)
                scores[j, some] = e
                total += e.reshape(BLK // 8, 8, tok).sum(0)
                delta += (e * d_weights[j, some]).reshape(BLK // 8, 8, tok).sum(0)
            stats[slot, j, 0:1] = top
            stats[slot, j, 1:2] = total.sum(0, keepdims=True)
            stats[slot, j, 2:3] = delta.sum(0, keepdims=True)

    meet(1, own0, tok)

    my_piece = pl.ds(pl.multiple_of(x * piece, piece), piece)

    def gather_copy(off):
        return remote(
            win.at[:, my_piece, :], win.at[:, my_piece, :],
            gather_send.at[off], gather_recv.at[x], y * ROW + lax.rem(xc + off, ROW), head,
        )

    def gather_got(slot):
        rows = win.at[:, slot * piece : (slot + 1) * piece, :]
        return remote(rows, rows, gather_send.at[0], gather_recv.at[slot], leaf, head)

    @pl.when(core == 0)
    def _():
        pl.when(leaf > 0)(lambda: root_copy(leaf).wait_recv())
        for off in range(1, ROW):
            gather_copy(off).start()

    def gather_done():
        for off in range(1, ROW):
            gather_copy(off).wait_send()

    pending.append(lambda: pl.when(core == 0)(gather_done))

    @pl.when(leaf >= 2)
    def _():
        for part in range(parts):
            shift_copy(2, part).wait_recv()
            swap_copy(part).start()

    def swap_done():
        for part in range(parts):
            swap_copy(part).wait_send()

    pending.append(lambda: pl.when(leaf >= 2)(swap_done))
    meet(3, own0 - 2 * tok, tok)

    for off in (1, 3):
        @pl.when(leaf >= off)
        def _():
            for part in range(parts):
                shift_copy(off, part).wait_recv()

        meet(off + 1, own0 - off * tok, tok)
    for slot in range(chips):
        pl.when((core == 1) | (x != slot))(lambda slot=slot: gather_got(slot).wait_recv())
    meet(0, 0, BLK)

    for j in range(heads_here):
        tops = [stats[slot, j, 0:1] for slot in range(REACH + 1)]
        top = functools.reduce(jnp.maximum, tops)
        scales = [jnp.exp2(t - top) for t in tops]
        inverse = 1.0 / sum(stats[slot, j, 1:2] * scales[slot] for slot in range(REACH + 1))
        stats[0, j, 4:5] = inverse * sum(stats[slot, j, 2:3] * scales[slot] for slot in range(REACH + 1))
        for slot in range(REACH + 1):
            stats[slot, j, 3:4] = inverse * scales[slot]

    def grad_of(slot, first, count):
        for j in range(heads_here):
            factor, delta = stats[slot, j, 3:4], stats[0, j, 4:5]
            for r in range(0, count, BLK):
                some = pl.ds(pl.multiple_of(first + r, BLK), BLK)
                w = scores[j, some] * factor
                probs[0, j, some] = w.astype(jnp.bfloat16)
                probs[1, j, some] = (w * (d_weights[j, some] - delta)).astype(jnp.bfloat16)
        rows = pl.ds(pl.multiple_of(first, BLK), count)
        dk = jnp.zeros((count, HD), jnp.float32)
        dv = jnp.zeros((count, HD), jnp.float32)
        for j in range(heads_here):
            cols = slice(j * HD, (j + 1) * HD)
            dk += dot(probs[1, j, rows], q[:, cols], NN)
            dv += dot(probs[0, j, rows], g[:, cols], NN)
        return dk * inv_scale, dv

    def rx_copy(slot):
        return remote(
            prompt_bf.at[:, slot * piece : (slot + 1) * piece, :], part_x.at[xc],
            rx_send.at[slot], rx_recv.at[xc], y * ROW + 2 * slot, head,
        )

    def rx_got(slot):
        return remote(part_x.at[slot], part_x.at[slot], rx_send.at[0], rx_recv.at[slot], leaf, head)

    dk, dv = grad_of(0, 0, BLK)
    prompt_grad[0], prompt_grad[1] = dk, dv
    prompt_bf[0], prompt_bf[1] = dk.astype(jnp.bfloat16), dv.astype(jnp.bfloat16)
    for slot in range(chips):
        pl.when(xc != 2 * slot)(lambda slot=slot: rx_copy(slot).start())
        pending.append(lambda slot=slot: pl.when(xc != 2 * slot)(lambda: rx_copy(slot).wait_send()))

    def grad_copy(slot, to):
        return remote(grads.at[slot], near.at[slot], grad_send.at[slot], grad_recv.at[slot], to, head)

    dk, dv = grad_of(side + 1, own0 - side * tok, tok)
    grads[0, 0], grads[0, 1] = dk.astype(jnp.bfloat16), dv.astype(jnp.bfloat16)
    pl.when(leaf >= 2)(lambda: grad_copy(0, sibling).start())
    pending.append(lambda: pl.when(leaf >= 2)(lambda: grad_copy(0, sibling).wait_send()))

    rest = REACH - side
    dk, dv = grad_of(rest + 1, own0 - rest * tok, tok)
    grads[2, 0], grads[2, 1] = dk.astype(jnp.bfloat16), dv.astype(jnp.bfloat16)
    pl.when(leaf >= rest)(lambda: grad_copy(2, leaf - rest).start())
    pending.append(lambda: pl.when(leaf >= rest)(lambda: grad_copy(2, leaf - rest).wait_send()))

    own_grad[0], own_grad[1] = grad_of(3, own0 - 2 * tok, tok)

    @pl.when(leaf >= 2)
    def _():
        grad_copy(0, sibling).wait_recv()
        grads[1] = (own_grad[...] + near[0].astype(jnp.float32)).astype(jnp.bfloat16)
        grad_copy(1, leaf - 2).start()

    pending.append(lambda: pl.when(leaf >= 2)(lambda: grad_copy(1, leaf - 2).wait_send()))

    def rr_copy():
        return remote(sum_x, part_root.at[leaf // 2], rr_send, rr_recv, 0, head)

    @pl.when(core == 0)
    def _():
        sum_all = prompt_grad[:, my_piece, :]
        for off in range(1, ROW):
            slot = lax.rem(xc + off, ROW)
            rx_got(slot).wait_recv()
            sum_all += part_x[slot].astype(jnp.float32)
        sum_x[...] = sum_all.astype(jnp.bfloat16)
        pl.when(leaf > 0)(lambda: rr_copy().start())

    pending.append(lambda: pl.when((core == 0) & (leaf > 0))(lambda: rr_copy().wait_send()))

    own_grad[0], own_grad[1] = grad_of(1, own0, tok)

    win_t[0] = win[0].T
    win_t[1] = win[1].T
    for j in range(heads_here):
        cols = slice(j * HD, (j + 1) * HD)
        attn[:, cols] = dot(win_t[1], probs[0, j], NN).T.astype(jnp.bfloat16)
    out_copy = pltpu.make_async_copy(attn, attn_out, store_sem.at[0])
    out_copy.start()
    pending.append(out_copy.wait)
    for j in range(heads_here):
        cols = slice(j * HD, (j + 1) * HD)
        dq[:, cols] = (dot(win_t[0], probs[1, j], NN).T * inv_scale).astype(jnp.bfloat16)
    dq_copy = pltpu.make_async_copy(dq, query_grad, store_sem.at[1])
    dq_copy.start()
    pending.append(dq_copy.wait)

    for slot, off in ((1, 2), (2, side)):
        @pl.when(leaf + off < leaves)
        def _():
            grad_copy(slot, leaf).wait_recv()
            own_grad[...] += near[slot].astype(jnp.float32)

    @pl.when(leaf == 0)
    def _():
        others = part_root.at[pl.ds(1, rows_y * chips - 1)]
        remote(others, others, rr_send, rr_recv, leaf, head).wait_recv()
        part_root[0] = sum_x[...]
        for slot in range(chips):
            rows = slice(slot * piece, (slot + 1) * piece)
            for row in range(rows_y):
                own_grad[:, rows, :] += part_root[row * chips + slot].astype(jnp.float32)

    final[...] = own_grad[...].astype(jnp.bfloat16)
    last = [
        pltpu.make_async_copy(final.at[0], key_grad, store_sem.at[2]),
        pltpu.make_async_copy(final.at[1], value_grad, store_sem.at[3]),
    ]
    for copy in last:
        copy.start()
        pending.append(copy.wait)

    for wait in pending:
        wait()


def store(*refs):
    copies = [pltpu.make_async_copy(refs[i], refs[4 + i], refs[8].at[i]) for i in range(4)]
    for copy in copies:
        copy.start()
    for copy in copies:
        copy.wait()


def on_device(leaves, groups, queries, key_rows, value_rows, out_grad, ancestry, block_fill):
    tok, width = queries.shape
    heads_here = width // HD
    wide = BLK + REACH * tok
    chips = ROW // 2
    piece = BLK // chips
    bf16, f32 = jnp.bfloat16, jnp.float32
    anywhere = pl.BlockSpec(memory_space=pl.ANY)
    in_hbm = pl.BlockSpec(memory_space=pltpu.HBM)
    dma = pltpu.SemaphoreType.DMA
    held = pl.pallas_call(
        functools.partial(kernel, leaves, groups),
        out_shape=(
            pltpu.VMEM((tok, width), bf16),
            pltpu.VMEM((tok, width), bf16),
            pltpu.VMEM((tok, HD), bf16),
            pltpu.VMEM((tok, HD), bf16),
        ),
        in_specs=[in_hbm] * 6,
        out_specs=(anywhere,) * 4,
        scratch_shapes=[
            pltpu.VMEM((tok, width), bf16),
            pltpu.VMEM((tok, width), bf16),
            pltpu.VMEM((2,) + key_rows.shape, bf16),
            pltpu.VMEM((2, wide, HD), bf16),
            pltpu.VMEM((2, HD, wide), bf16),
            pltpu.VMEM((wide, tok), f32),
            pltpu.VMEM((heads_here, wide, tok), f32),
            pltpu.VMEM((heads_here, wide, tok), f32),
            pltpu.VMEM((REACH + 1, heads_here, 8, tok), f32),
            pltpu.VMEM((2, heads_here, wide, tok), bf16),
            pltpu.VMEM((tok, width), bf16),
            pltpu.VMEM((tok, width), bf16),
            pltpu.VMEM((REACH, 2, tok, HD), bf16),
            pltpu.VMEM((2, tok, HD), f32),
            pltpu.VMEM((2, BLK, HD), f32),
            pltpu.VMEM((2, BLK, HD), bf16),
            pltpu.VMEM((REACH, 2, tok, HD), bf16),
            pltpu.VMEM((ROW, 2, piece, HD), bf16),
            pltpu.VMEM((2, piece, HD), bf16),
            pltpu.VMEM((leaves // 2, 2, piece, HD), bf16),
            pltpu.VMEM((2, tok, HD), bf16),
            pltpu.SMEM((8, ancestry.shape[1]), jnp.int32),
            pltpu.SMEM(block_fill.shape, jnp.int32),
            dma((6,)),
            dma((4,)),
            dma((groups,)),
            dma((groups,)),
            dma((REACH, max(1, groups // 2))),
            dma((REACH, max(1, groups // 2))),
            dma((leaves,)),
            dma,
            dma((ROW,)),
            dma((ROW,)),
            dma((REACH,)),
            dma((REACH,)),
            dma((ROW,)),
            dma((ROW,)),
            dma,
            dma,
            pltpu.SemaphoreType.REGULAR,
        ],
        compiler_params=pltpu.CompilerParams(
            collective_id=0, has_side_effects=True, vmem_limit_bytes=50 * 2**20
        ),
    )(
        *(
            pltpu.with_memory_space_constraint(a, pltpu.HBM)
            for a in (queries, key_rows, value_rows, out_grad, ancestry, block_fill)
        )
    )
    return pl.pallas_call(
        store,
        out_shape=[jax.ShapeDtypeStruct(a.shape, a.dtype) for a in held],
        in_specs=[anywhere] * 4,
        out_specs=[in_hbm] * 4,
        scratch_shapes=[dma((4,))],
    )(*(pltpu.with_memory_space_constraint(a, pltpu.VMEM) for a in held))


def solution(mesh):
    placed = (
        P("leaf", "head"),
        P(("leaf", "head"), None),
        P(("leaf", "head"), None),
        P("leaf", "head"),
        P(),
        P(),
    )
    return jax.shard_map(
        functools.partial(on_device, mesh.shape["leaf"], mesh.shape["head"]),
        mesh=mesh,
        in_specs=placed,
        out_specs=(P("leaf", "head"), P("leaf", "head"), P("leaf", "head"), P("leaf", "head")),
        check_vma=False,
    )
```

```python
import functools
import math

import jax
import jax.numpy as jnp
from jax import lax
from jax.experimental import pallas as pl
from jax.experimental.pallas import tpu as pltpu
from jax.sharding import PartitionSpec as P

HD = 128
BLK = 128
REACH = 4
ROW = 8
MESH = pl.DeviceIdType.MESH
NEG = -1e30
NT = (((1,), (1,)), ((), ()))
NN = (((1,), (0,)), ((), ()))
dot = functools.partial(lax.dot_general, preferred_element_type=jnp.float32)


def kernel(
    leaves, groups, queries, key_rows, value_rows, out_grad, ancestry, fills,
    attn_out, query_grad, key_grad, value_grad,
    q, g, kv_in, win, win_t, bias, scores, d_weights, stats, probs, attn, dq,
    grads, own_grad, prompt_grad, prompt_bf, near, part_x, sum_x, part_root,
    final, anc, block_fill,
    load_sem, store_sem, a2a_send, a2a_recv, shift_send, shift_recv, root_send, root_recv,
    gather_send, gather_recv, grad_send, grad_recv, rx_send, rx_recv, rr_send, rr_recv, ready, zready,
):
    leaf = lax.axis_index("leaf")
    head = lax.axis_index("head")
    tok = q.shape[0]
    heads_here = q.shape[1] // HD
    rows_in = kv_in.shape[1]
    rows_y = leaves // ROW
    chips = ROW // 2
    piece = BLK // chips
    wide = win.shape[1]
    own0 = wide - tok
    y = leaf // ROW
    xc = leaf % ROW
    x = xc // 2
    core = leaf % 2
    sibling = leaf + 1 - 2 * core
    half = groups // 2
    lower = head < half
    inv_scale = 1.0 / math.sqrt(HD)
    log_scale = inv_scale * math.log2(math.e)

    base = pl.multiple_of((2 * leaf) // 8 * 8, 8)
    loads = [
        pltpu.make_async_copy(key_rows, kv_in.at[0], load_sem.at[0]),
        pltpu.make_async_copy(value_rows, kv_in.at[1], load_sem.at[1]),
        pltpu.make_async_copy(queries, q, load_sem.at[2]),
        pltpu.make_async_copy(out_grad, g, load_sem.at[3]),
        pltpu.make_async_copy(ancestry.at[pl.ds(base, 8)], anc, load_sem.at[4]),
        pltpu.make_async_copy(fills, block_fill, load_sem.at[5]),
    ]
    for load in loads[:2]:
        load.start()

    pending = []
    barrier = pltpu.get_barrier_semaphore()

    def greet(leaf_to, head_to):
        pl.semaphore_signal(barrier, inc=1, device_id=(leaf_to, head_to), device_id_type=MESH)

    for off in range(1, groups):
        to = lax.rem(head + off, groups)
        pl.when(lower | (to >= half))(functools.partial(greet, leaf, to))
    for off in range(1, ROW):
        greet(y * ROW + lax.rem(xc + off, ROW), head)
    for off in range(1, REACH):
        pl.when(leaf >= off)(functools.partial(greet, leaf - off, head))
        pl.when(leaf + off < leaves)(functools.partial(greet, leaf + off, head))

    @pl.when(leaf == 0)
    def _():
        @pl.loop(1, leaves)
        def _(to):
            greet(to, head)

    for load in loads[:2]:
        load.wait()
    greeted = jnp.where(lower, half, groups) - 1 + ROW - 1 + jnp.minimum(leaf, REACH - 1) + jnp.minimum(leaves - 1 - leaf, REACH - 1)
    greeted += jnp.where(leaf == 0, 0, 1)
    pl.semaphore_wait(barrier, greeted)

    @pl.when((leaf > 0) & (core == 0))
    def _():
        pl.semaphore_signal(ready, inc=1, device_id=(0, head), device_id_type=MESH)

    @pl.when(head >= half)
    def _():
        for to in range(half):
            pl.semaphore_signal(zready, inc=1, device_id=(leaf, to), device_id_type=MESH)

    def remote(src, dst, send, recv, leaf_to, head_to):
        return pltpu.make_async_remote_copy(
            src_ref=src, dst_ref=dst, send_sem=send, recv_sem=recv,
            device_id=(leaf_to, head_to), device_id_type=MESH,
        )

    def a2a_copy(off):
        to = lax.rem(head + off, groups)
        return remote(
            kv_in.at[:, :, pl.ds(pl.multiple_of(to * HD, HD), HD)],
            win.at[:, pl.ds(pl.multiple_of(own0 + head * rows_in, 32), rows_in), :],
            a2a_send.at[off], a2a_recv.at[off], leaf, to,
        )

    for off in range(1, groups):
        to = lax.rem(head + off, groups)
        pl.when((head >= half) | (to < half))(lambda off=off: a2a_copy(off).start())
        pending.append(a2a_copy(off).wait_send)
    for load in loads[2:]:
        load.start()
    win[:, pl.ds(pl.multiple_of(own0 + head * rows_in, 32), rows_in), :] = kv_in[
        :, :, pl.ds(pl.multiple_of(head * HD, HD), HD)
    ]
    for off in range(1, REACH):
        rows = pl.ds(own0 - off * tok, tok)

        @pl.when(leaf < off)
        def _():
            win[:, rows, :] = jnp.zeros((2, tok, HD), win.dtype)

    loads[4].wait()
    loads[5].wait()
    key_iota = lax.broadcasted_iota(jnp.int32, (BLK, BLK), 0)
    query_iota = lax.broadcasted_iota(jnp.int32, (BLK, BLK), 1)
    blocks_dev = tok // BLK
    for col in range(wide // BLK):
        block = 0 if col == 0 else (leaf - (REACH - 1)) * blocks_dev + col - 1
        at = 0 if col == 0 else jnp.maximum(block, 0)
        fill = block_fill[at]
        for row in range(blocks_dev):
            link = anc[2 * leaf - base + row, at]
            if col > 0:
                link = jnp.where(block >= 1, link, 0)
            limit = jnp.where(link == 1, fill, 0)
            allowed = (key_iota < limit) & (
                key_iota + block * BLK <= query_iota + (leaf * blocks_dev + row) * BLK
            )
            bias[col * BLK : (col + 1) * BLK, row * BLK : (row + 1) * BLK] = jnp.where(allowed, 0.0, NEG)

    side = jnp.where(core == 0, 1, REACH - 1)

    parts = max(1, groups // 2)
    part_rows = tok // parts

    def part_of(off, part):
        return win.at[:, pl.ds(pl.multiple_of(own0 - off * tok + part * part_rows, 32), part_rows), :]

    def shift_copy(off, part):
        return remote(
            part_of(0, part), part_of(off, part),
            shift_send.at[off, part], shift_recv.at[off, part], leaf + off, head,
        )

    def swap_copy(part):
        lands = REACH - side
        return remote(
            part_of(2, part), part_of(lands, part),
            shift_send.at[0, part], shift_recv.at[lands, part], sibling, head,
        )

    def root_copy(to):
        at = to % ROW // 2 * piece
        return remote(
            win.at[:, pl.ds(pl.multiple_of(own0 + at, piece), piece), :],
            win.at[:, pl.ds(pl.multiple_of(at, piece), piece), :],
            root_send.at[to], root_recv, to, head,
        )

    def scatter():
        pl.semaphore_wait(ready, rows_y * chips - 1)
        for row in sorted(range(rows_y), key=lambda r: -min(r, rows_y - r)):
            @pl.loop(int(row == 0), chips)
            def _(i):
                root_copy(row * ROW + 2 * i).start()

        win[:, :piece, :] = win[:, own0 : own0 + piece, :]

    def send_upper():
        pl.semaphore_wait(zready, groups - half)
        for to in range(half, groups):
            a2a_copy(to - head).start()

    per_part = groups // parts
    for part in range(parts):
        for source in range(part * per_part, (part + 1) * per_part):
            off = lax.rem(head - source + groups, groups)
            pl.when(off > 0)(lambda off=off: a2a_copy(off).wait_recv())
        for off in (2, side):
            pl.when(leaf + off < leaves)(lambda off=off: shift_copy(off, part).start())
        if part * part_rows < BLK <= (part + 1) * part_rows:
            pl.when(leaf == 0)(scatter)
            pl.when(lower)(send_upper)

    def shift_done():
        for part in range(parts):
            for off in (2, side):
                pl.when(leaf + off < leaves)(lambda off=off: shift_copy(off, part).wait_send())

    pending.append(shift_done)

    def root_done():
        @pl.when(leaf == 0)
        def _():
            @pl.loop(1, rows_y * chips)
            def _(i):
                root_copy(2 * i).wait_send()

    pending.append(root_done)

    loads[2].wait()
    loads[3].wait()

    def meet(slot, first, count):
        rows = slice(first, first + count)
        keys, values, added = win[0, rows], win[1, rows], bias[rows]
        for j in range(heads_here):
            cols = slice(j * HD, (j + 1) * HD)
            part = dot(keys, q[:, cols], NT) + added
            scores[j, rows] = part
            top = part.reshape(count // 8, 8, tok).max(0).max(0, keepdims=True) * log_scale
            d_weights[j, rows] = dot(values, g[:, cols], NT)
            total = jnp.zeros((8, tok), jnp.float32)
            delta = jnp.zeros((8, tok), jnp.float32)
            for r in range(first, first + count, BLK):
                some = slice(r, r + BLK)
                e = jnp.exp2(scores[j, some] * log_scale - top)
                scores[j, some] = e
                total += e.reshape(BLK // 8, 8, tok).sum(0)
                delta += (e * d_weights[j, some]).reshape(BLK // 8, 8, tok).sum(0)
            stats[slot, j, 0:1] = top
            stats[slot, j, 1:2] = total.sum(0, keepdims=True)
            stats[slot, j, 2:3] = delta.sum(0, keepdims=True)

    meet(1, own0, tok)

    my_piece = pl.ds(pl.multiple_of(x * piece, piece), piece)

    def gather_copy(off):
        return remote(
            win.at[:, my_piece, :], win.at[:, my_piece, :],
            gather_send.at[off], gather_recv.at[x], y * ROW + lax.rem(xc + off, ROW), head,
        )

    def gather_got(slot):
        rows = win.at[:, slot * piece : (slot + 1) * piece, :]
        return remote(rows, rows, gather_send.at[0], gather_recv.at[slot], leaf, head)

    @pl.when(core == 0)
    def _():
        pl.when(leaf > 0)(lambda: root_copy(leaf).wait_recv())
        for off in range(1, ROW):
            gather_copy(off).start()

    def gather_done():
        for off in range(1, ROW):
            gather_copy(off).wait_send()

    pending.append(lambda: pl.when(core == 0)(gather_done))

    @pl.when(leaf >= 2)
    def _():
        for part in range(parts):
            shift_copy(2, part).wait_recv()
            swap_copy(part).start()

    def swap_done():
        for part in range(parts):
            swap_copy(part).wait_send()

    pending.append(lambda: pl.when(leaf >= 2)(swap_done))
    meet(3, own0 - 2 * tok, tok)

    for off in (1, 3):
        @pl.when(leaf >= off)
        def _():
            for part in range(parts):
                shift_copy(off, part).wait_recv()

        meet(off + 1, own0 - off * tok, tok)
    for slot in range(chips):
        pl.when((core == 1) | (x != slot))(lambda slot=slot: gather_got(slot).wait_recv())
    meet(0, 0, BLK)

    for j in range(heads_here):
        tops = [stats[slot, j, 0:1] for slot in range(REACH + 1)]
        top = functools.reduce(jnp.maximum, tops)
        scales = [jnp.exp2(t - top) for t in tops]
        inverse = 1.0 / sum(stats[slot, j, 1:2] * scales[slot] for slot in range(REACH + 1))
        stats[0, j, 4:5] = inverse * sum(stats[slot, j, 2:3] * scales[slot] for slot in range(REACH + 1))
        for slot in range(REACH + 1):
            stats[slot, j, 3:4] = inverse * scales[slot]

    def grad_of(slot, first, count):
        for j in range(heads_here):
            factor, delta = stats[slot, j, 3:4], stats[0, j, 4:5]
            for r in range(0, count, BLK):
                some = pl.ds(pl.multiple_of(first + r, BLK), BLK)
                w = scores[j, some] * factor
                probs[0, j, some] = w.astype(jnp.bfloat16)
                probs[1, j, some] = (w * (d_weights[j, some] - delta)).astype(jnp.bfloat16)
        rows = pl.ds(pl.multiple_of(first, BLK), count)
        dk = jnp.zeros((count, HD), jnp.float32)
        dv = jnp.zeros((count, HD), jnp.float32)
        for j in range(heads_here):
            cols = slice(j * HD, (j + 1) * HD)
            dk += dot(probs[1, j, rows], q[:, cols], NN)
            dv += dot(probs[0, j, rows], g[:, cols], NN)
        return dk * inv_scale, dv

    def rx_copy(slot):
        return remote(
            prompt_bf.at[:, slot * piece : (slot + 1) * piece, :], part_x.at[xc],
            rx_send.at[slot], rx_recv.at[xc], y * ROW + 2 * slot, head,
        )

    def rx_got(slot):
        return remote(part_x.at[slot], part_x.at[slot], rx_send.at[0], rx_recv.at[slot], leaf, head)

    dk, dv = grad_of(0, 0, BLK)
    prompt_grad[0], prompt_grad[1] = dk, dv
    prompt_bf[0], prompt_bf[1] = dk.astype(jnp.bfloat16), dv.astype(jnp.bfloat16)
    for slot in range(chips):
        pl.when(xc != 2 * slot)(lambda slot=slot: rx_copy(slot).start())
        pending.append(lambda slot=slot: pl.when(xc != 2 * slot)(lambda: rx_copy(slot).wait_send()))

    def grad_copy(slot, to):
        return remote(grads.at[slot], near.at[slot], grad_send.at[slot], grad_recv.at[slot], to, head)

    dk, dv = grad_of(side + 1, own0 - side * tok, tok)
    grads[0, 0], grads[0, 1] = dk.astype(jnp.bfloat16), dv.astype(jnp.bfloat16)
    pl.when(leaf >= 2)(lambda: grad_copy(0, sibling).start())
    pending.append(lambda: pl.when(leaf >= 2)(lambda: grad_copy(0, sibling).wait_send()))

    rest = REACH - side
    dk, dv = grad_of(rest + 1, own0 - rest * tok, tok)
    grads[2, 0], grads[2, 1] = dk.astype(jnp.bfloat16), dv.astype(jnp.bfloat16)
    pl.when(leaf >= rest)(lambda: grad_copy(2, leaf - rest).start())
    pending.append(lambda: pl.when(leaf >= rest)(lambda: grad_copy(2, leaf - rest).wait_send()))

    own_grad[0], own_grad[1] = grad_of(3, own0 - 2 * tok, tok)

    @pl.when(leaf >= 2)
    def _():
        grad_copy(0, sibling).wait_recv()
        grads[1] = (own_grad[...] + near[0].astype(jnp.float32)).astype(jnp.bfloat16)
        grad_copy(1, leaf - 2).start()

    pending.append(lambda: pl.when(leaf >= 2)(lambda: grad_copy(1, leaf - 2).wait_send()))

    def rr_copy():
        return remote(sum_x, part_root.at[leaf // 2], rr_send, rr_recv, 0, head)

    @pl.when(core == 0)
    def _():
        sum_all = prompt_grad[:, my_piece, :]
        for off in range(1, ROW):
            slot = lax.rem(xc + off, ROW)
            rx_got(slot).wait_recv()
            sum_all += part_x[slot].astype(jnp.float32)
        sum_x[...] = sum_all.astype(jnp.bfloat16)
        pl.when(leaf > 0)(lambda: rr_copy().start())

    pending.append(lambda: pl.when((core == 0) & (leaf > 0))(lambda: rr_copy().wait_send()))

    own_grad[0], own_grad[1] = grad_of(1, own0, tok)

    win_t[0] = win[0].T
    win_t[1] = win[1].T
    for j in range(heads_here):
        cols = slice(j * HD, (j + 1) * HD)
        attn[:, cols] = dot(win_t[1], probs[0, j], NN).T.astype(jnp.bfloat16)
    out_copy = pltpu.make_async_copy(attn, attn_out, store_sem.at[0])
    out_copy.start()
    pending.append(out_copy.wait)
    for j in range(heads_here):
        cols = slice(j * HD, (j + 1) * HD)
        dq[:, cols] = (dot(win_t[0], probs[1, j], NN).T * inv_scale).astype(jnp.bfloat16)
    dq_copy = pltpu.make_async_copy(dq, query_grad, store_sem.at[1])
    dq_copy.start()
    pending.append(dq_copy.wait)

    for slot, off in ((1, 2), (2, side)):
        @pl.when(leaf + off < leaves)
        def _():
            grad_copy(slot, leaf).wait_recv()
            own_grad[...] += near[slot].astype(jnp.float32)

    @pl.when(leaf == 0)
    def _():
        others = part_root.at[pl.ds(1, rows_y * chips - 1)]
        remote(others, others, rr_send, rr_recv, leaf, head).wait_recv()
        part_root[0] = sum_x[...]
        for slot in range(chips):
            rows = slice(slot * piece, (slot + 1) * piece)
            for row in range(rows_y):
                own_grad[:, rows, :] += part_root[row * chips + slot].astype(jnp.float32)

    final[...] = own_grad[...].astype(jnp.bfloat16)
    last = [
        pltpu.make_async_copy(final.at[0], key_grad, store_sem.at[2]),
        pltpu.make_async_copy(final.at[1], value_grad, store_sem.at[3]),
    ]
    for copy in last:
        copy.start()
        pending.append(copy.wait)

    for wait in pending:
        wait()


def store(*refs):
    copies = [pltpu.make_async_copy(refs[i], refs[4 + i], refs[8].at[i]) for i in range(4)]
    for copy in copies:
        copy.start()
    for copy in copies:
        copy.wait()


def on_device(leaves, groups, queries, key_rows, value_rows, out_grad, ancestry, block_fill):
    tok, width = queries.shape
    heads_here = width // HD
    wide = BLK + REACH * tok
    chips = ROW // 2
    piece = BLK // chips
    bf16, f32 = jnp.bfloat16, jnp.float32
    anywhere = pl.BlockSpec(memory_space=pl.ANY)
    in_hbm = pl.BlockSpec(memory_space=pltpu.HBM)
    dma = pltpu.SemaphoreType.DMA
    held = pl.pallas_call(
        functools.partial(kernel, leaves, groups),
        out_shape=(
            pltpu.VMEM((tok, width), bf16),
            pltpu.VMEM((tok, width), bf16),
            pltpu.VMEM((tok, HD), bf16),
            pltpu.VMEM((tok, HD), bf16),
        ),
        in_specs=[in_hbm] * 6,
        out_specs=(anywhere,) * 4,
        scratch_shapes=[
            pltpu.VMEM((tok, width), bf16),
            pltpu.VMEM((tok, width), bf16),
            pltpu.VMEM((2,) + key_rows.shape, bf16),
            pltpu.VMEM((2, wide, HD), bf16),
            pltpu.VMEM((2, HD, wide), bf16),
            pltpu.VMEM((wide, tok), f32),
            pltpu.VMEM((heads_here, wide, tok), f32),
            pltpu.VMEM((heads_here, wide, tok), f32),
            pltpu.VMEM((REACH + 1, heads_here, 8, tok), f32),
            pltpu.VMEM((2, heads_here, wide, tok), bf16),
            pltpu.VMEM((tok, width), bf16),
            pltpu.VMEM((tok, width), bf16),
            pltpu.VMEM((REACH, 2, tok, HD), bf16),
            pltpu.VMEM((2, tok, HD), f32),
            pltpu.VMEM((2, BLK, HD), f32),
            pltpu.VMEM((2, BLK, HD), bf16),
            pltpu.VMEM((REACH, 2, tok, HD), bf16),
            pltpu.VMEM((ROW, 2, piece, HD), bf16),
            pltpu.VMEM((2, piece, HD), bf16),
            pltpu.VMEM((leaves // 2, 2, piece, HD), bf16),
            pltpu.VMEM((2, tok, HD), bf16),
            pltpu.SMEM((8, ancestry.shape[1]), jnp.int32),
            pltpu.SMEM(block_fill.shape, jnp.int32),
            dma((6,)),
            dma((4,)),
            dma((groups,)),
            dma((groups,)),
            dma((REACH, max(1, groups // 2))),
            dma((REACH, max(1, groups // 2))),
            dma((leaves,)),
            dma,
            dma((ROW,)),
            dma((ROW,)),
            dma((REACH,)),
            dma((REACH,)),
            dma((ROW,)),
            dma((ROW,)),
            dma,
            dma,
            pltpu.SemaphoreType.REGULAR,
            pltpu.SemaphoreType.REGULAR,
        ],
        compiler_params=pltpu.CompilerParams(
            collective_id=0, has_side_effects=True, vmem_limit_bytes=50 * 2**20
        ),
    )(
        *(
            pltpu.with_memory_space_constraint(a, pltpu.HBM)
            for a in (queries, key_rows, value_rows, out_grad, ancestry, block_fill)
        )
    )
    return pl.pallas_call(
        store,
        out_shape=[jax.ShapeDtypeStruct(a.shape, a.dtype) for a in held],
        in_specs=[anywhere] * 4,
        out_specs=[in_hbm] * 4,
        scratch_shapes=[dma((4,))],
    )(*(pltpu.with_memory_space_constraint(a, pltpu.VMEM) for a in held))


def solution(mesh):
    placed = (
        P("leaf", "head"),
        P(("leaf", "head"), None),
        P(("leaf", "head"), None),
        P("leaf", "head"),
        P(),
        P(),
    )
    return jax.shard_map(
        functools.partial(on_device, mesh.shape["leaf"], mesh.shape["head"]),
        mesh=mesh,
        in_specs=placed,
        out_specs=(P("leaf", "head"), P("leaf", "head"), P("leaf", "head"), P("leaf", "head")),
        check_vma=False,
    )
```

```python
import functools
import math

import jax
import jax.numpy as jnp
from jax import lax
from jax.experimental import pallas as pl
from jax.experimental.pallas import tpu as pltpu
from jax.sharding import PartitionSpec as P

HD = 128
BLK = 128
REACH = 4
ROW = 8
HOLDERS = (0, 1, 2, 6)
MESH = pl.DeviceIdType.MESH
NEG = -1e30
NT = (((1,), (1,)), ((), ()))
NN = (((1,), (0,)), ((), ()))
dot = functools.partial(lax.dot_general, preferred_element_type=jnp.float32)


def kernel(
    leaves, groups, queries, key_rows, value_rows, out_grad, ancestry, fills,
    attn_out, query_grad, key_grad, value_grad,
    q, g, kv_in, win, win_t, bias, scores, d_weights, stats, probs, attn, dq,
    grads, own_grad, prompt_grad, prompt_bf, near, part_x, sum_x, part_root,
    anc, block_fill,
    load_sem, store_sem, a2a_send, a2a_recv, shift_send, shift_recv, root_send, root_recv,
    gather_send, gather_recv, grad_send, grad_recv, rx_send, rx_recv, rr_send, rr_recv, ready, zready,
):
    leaf = lax.axis_index("leaf")
    head = lax.axis_index("head")
    tok = q.shape[0]
    heads_here = q.shape[1] // HD
    rows_in = kv_in.shape[1]
    rows_y = leaves // ROW
    chips = ROW // 2
    piece = BLK // chips
    wide = win.shape[1]
    own0 = wide - tok
    y = leaf // ROW
    xc = leaf % ROW
    x = xc // 2
    core = leaf % 2
    sibling = leaf + 1 - 2 * core
    half = groups // 2
    lower = head < half
    inv_scale = 1.0 / math.sqrt(HD)
    log_scale = inv_scale * math.log2(math.e)

    base = pl.multiple_of((2 * leaf) // 8 * 8, 8)
    loads = [
        pltpu.make_async_copy(key_rows, kv_in.at[0], load_sem.at[0]),
        pltpu.make_async_copy(value_rows, kv_in.at[1], load_sem.at[1]),
        pltpu.make_async_copy(queries, q, load_sem.at[2]),
        pltpu.make_async_copy(out_grad, g, load_sem.at[3]),
        pltpu.make_async_copy(ancestry.at[pl.ds(base, 8)], anc, load_sem.at[4]),
        pltpu.make_async_copy(fills, block_fill, load_sem.at[5]),
    ]
    for load in loads[:2]:
        load.start()

    pending = []
    barrier = pltpu.get_barrier_semaphore()

    def greet(leaf_to, head_to):
        pl.semaphore_signal(barrier, inc=1, device_id=(leaf_to, head_to), device_id_type=MESH)

    for off in range(1, groups):
        to = lax.rem(head + off, groups)
        pl.when(lower | (to >= half))(functools.partial(greet, leaf, to))
    for off in range(1, ROW):
        greet(y * ROW + lax.rem(xc + off, ROW), head)
    for off in range(1, REACH):
        pl.when(leaf >= off)(functools.partial(greet, leaf - off, head))
        pl.when(leaf + off < leaves)(functools.partial(greet, leaf + off, head))

    @pl.when(leaf == 0)
    def _():
        @pl.loop(1, leaves)
        def _(to):
            greet(to, head)

    for load in loads[:2]:
        load.wait()
    greeted = jnp.where(lower, half, groups) - 1 + ROW - 1 + jnp.minimum(leaf, REACH - 1) + jnp.minimum(leaves - 1 - leaf, REACH - 1)
    greeted += jnp.where(leaf == 0, 0, 1)
    pl.semaphore_wait(barrier, greeted)

    @pl.when((leaf > 0) & (core == 0))
    def _():
        pl.semaphore_signal(ready, inc=1, device_id=(0, head), device_id_type=MESH)

    @pl.when(head >= half)
    def _():
        for to in range(half):
            pl.semaphore_signal(zready, inc=1, device_id=(leaf, to), device_id_type=MESH)

    def remote(src, dst, send, recv, leaf_to, head_to):
        return pltpu.make_async_remote_copy(
            src_ref=src, dst_ref=dst, send_sem=send, recv_sem=recv,
            device_id=(leaf_to, head_to), device_id_type=MESH,
        )

    def a2a_copy(off):
        to = lax.rem(head + off, groups)
        return remote(
            kv_in.at[:, :, pl.ds(pl.multiple_of(to * HD, HD), HD)],
            win.at[:, pl.ds(pl.multiple_of(own0 + head * rows_in, 32), rows_in), :],
            a2a_send.at[off], a2a_recv.at[off], leaf, to,
        )

    for off in range(1, groups):
        to = lax.rem(head + off, groups)
        pl.when((head >= half) | (to < half))(lambda off=off: a2a_copy(off).start())
        pending.append(a2a_copy(off).wait_send)
    for load in loads[2:]:
        load.start()
    win[:, pl.ds(pl.multiple_of(own0 + head * rows_in, 32), rows_in), :] = kv_in[
        :, :, pl.ds(pl.multiple_of(head * HD, HD), HD)
    ]
    for off in range(1, REACH):
        rows = pl.ds(own0 - off * tok, tok)

        @pl.when(leaf < off)
        def _():
            win[:, rows, :] = jnp.zeros((2, tok, HD), win.dtype)

    loads[4].wait()
    loads[5].wait()
    key_iota = lax.broadcasted_iota(jnp.int32, (BLK, BLK), 0)
    query_iota = lax.broadcasted_iota(jnp.int32, (BLK, BLK), 1)
    blocks_dev = tok // BLK
    for col in range(wide // BLK):
        block = 0 if col == 0 else (leaf - (REACH - 1)) * blocks_dev + col - 1
        at = 0 if col == 0 else jnp.maximum(block, 0)
        fill = block_fill[at]
        for row in range(blocks_dev):
            link = anc[2 * leaf - base + row, at]
            if col > 0:
                link = jnp.where(block >= 1, link, 0)
            limit = jnp.where(link == 1, fill, 0)
            allowed = (key_iota < limit) & (
                key_iota + block * BLK <= query_iota + (leaf * blocks_dev + row) * BLK
            )
            bias[col * BLK : (col + 1) * BLK, row * BLK : (row + 1) * BLK] = jnp.where(allowed, 0.0, NEG)

    side = jnp.where(core == 0, 1, REACH - 1)

    parts = max(1, groups // 2)
    part_rows = tok // parts

    def part_of(off, part):
        return win.at[:, pl.ds(pl.multiple_of(own0 - off * tok + part * part_rows, 32), part_rows), :]

    def shift_copy(off, part):
        return remote(
            part_of(0, part), part_of(off, part),
            shift_send.at[off, part], shift_recv.at[off, part], leaf + off, head,
        )

    def swap_copy(part):
        lands = REACH - side
        return remote(
            part_of(2, part), part_of(lands, part),
            shift_send.at[0, part], shift_recv.at[lands, part], sibling, head,
        )

    def root_copy(to):
        at = to % ROW // 2 * piece
        return remote(
            win.at[:, pl.ds(pl.multiple_of(own0 + at, piece), piece), :],
            win.at[:, pl.ds(pl.multiple_of(at, piece), piece), :],
            root_send.at[to], root_recv, to, head,
        )

    def scatter():
        pl.semaphore_wait(ready, rows_y * chips - 1)
        for row in sorted(range(rows_y), key=lambda r: -min(r, rows_y - r)):
            @pl.loop(int(row == 0), chips)
            def _(i):
                root_copy(row * ROW + 2 * i).start()

        win[:, :piece, :] = win[:, own0 : own0 + piece, :]

    def send_upper():
        pl.semaphore_wait(zready, groups - half)
        for to in range(half, groups):
            a2a_copy(to - head).start()

    per_part = groups // parts
    for part in range(parts):
        for source in range(part * per_part, (part + 1) * per_part):
            off = lax.rem(head - source + groups, groups)
            pl.when(off > 0)(lambda off=off: a2a_copy(off).wait_recv())
        for off in (2, side):
            pl.when(leaf + off < leaves)(lambda off=off: shift_copy(off, part).start())
        if part * part_rows < BLK <= (part + 1) * part_rows:
            pl.when(leaf == 0)(scatter)
            pl.when(lower)(send_upper)

    def shift_done():
        for part in range(parts):
            for off in (2, side):
                pl.when(leaf + off < leaves)(lambda off=off: shift_copy(off, part).wait_send())

    pending.append(shift_done)

    def root_done():
        @pl.when(leaf == 0)
        def _():
            @pl.loop(1, rows_y * chips)
            def _(i):
                root_copy(2 * i).wait_send()

    pending.append(root_done)

    loads[2].wait()
    loads[3].wait()

    def meet(slot, first, count):
        rows = slice(first, first + count)
        keys, values, added = win[0, rows], win[1, rows], bias[rows]
        for j in range(heads_here):
            cols = slice(j * HD, (j + 1) * HD)
            part = dot(keys, q[:, cols], NT) + added
            scores[j, rows] = part
            top = part.reshape(count // 8, 8, tok).max(0).max(0, keepdims=True) * log_scale
            d_weights[j, rows] = dot(values, g[:, cols], NT)
            total = jnp.zeros((8, tok), jnp.float32)
            delta = jnp.zeros((8, tok), jnp.float32)
            for r in range(first, first + count, BLK):
                some = slice(r, r + BLK)
                e = jnp.exp2(scores[j, some] * log_scale - top)
                scores[j, some] = e
                total += e.reshape(BLK // 8, 8, tok).sum(0)
                delta += (e * d_weights[j, some]).reshape(BLK // 8, 8, tok).sum(0)
            stats[slot, j, 0:1] = top
            stats[slot, j, 1:2] = total.sum(0, keepdims=True)
            stats[slot, j, 2:3] = delta.sum(0, keepdims=True)

    meet(1, own0, tok)

    my_piece = pl.ds(pl.multiple_of(x * piece, piece), piece)

    def gather_copy(off):
        return remote(
            win.at[:, my_piece, :], win.at[:, my_piece, :],
            gather_send.at[off], gather_recv.at[x], y * ROW + lax.rem(xc + off, ROW), head,
        )

    def gather_got(slot):
        rows = win.at[:, slot * piece : (slot + 1) * piece, :]
        return remote(rows, rows, gather_send.at[0], gather_recv.at[slot], leaf, head)

    @pl.when(core == 0)
    def _():
        pl.when(leaf > 0)(lambda: root_copy(leaf).wait_recv())
        for off in range(1, ROW):
            gather_copy(off).start()

    def gather_done():
        for off in range(1, ROW):
            gather_copy(off).wait_send()

    pending.append(lambda: pl.when(core == 0)(gather_done))

    @pl.when(leaf >= 2)
    def _():
        for part in range(parts):
            shift_copy(2, part).wait_recv()
            swap_copy(part).start()

    def swap_done():
        for part in range(parts):
            swap_copy(part).wait_send()

    pending.append(lambda: pl.when(leaf >= 2)(swap_done))
    meet(3, own0 - 2 * tok, tok)

    for off in (1, 3):
        @pl.when(leaf >= off)
        def _():
            for part in range(parts):
                shift_copy(off, part).wait_recv()

        meet(off + 1, own0 - off * tok, tok)
    for slot in range(chips):
        pl.when((core == 1) | (x != slot))(lambda slot=slot: gather_got(slot).wait_recv())
    meet(0, 0, BLK)

    for j in range(heads_here):
        tops = [stats[slot, j, 0:1] for slot in range(REACH + 1)]
        top = functools.reduce(jnp.maximum, tops)
        scales = [jnp.exp2(t - top) for t in tops]
        inverse = 1.0 / sum(stats[slot, j, 1:2] * scales[slot] for slot in range(REACH + 1))
        stats[0, j, 4:5] = inverse * sum(stats[slot, j, 2:3] * scales[slot] for slot in range(REACH + 1))
        for slot in range(REACH + 1):
            stats[slot, j, 3:4] = inverse * scales[slot]

    def grad_of(slot, first, count):
        for j in range(heads_here):
            factor, delta = stats[slot, j, 3:4], stats[0, j, 4:5]
            for r in range(0, count, BLK):
                some = pl.ds(pl.multiple_of(first + r, BLK), BLK)
                w = scores[j, some] * factor
                probs[0, j, some] = w.astype(jnp.bfloat16)
                probs[1, j, some] = (w * (d_weights[j, some] - delta)).astype(jnp.bfloat16)
        rows = pl.ds(pl.multiple_of(first, BLK), count)
        dk = jnp.zeros((count, HD), jnp.float32)
        dv = jnp.zeros((count, HD), jnp.float32)
        for j in range(heads_here):
            cols = slice(j * HD, (j + 1) * HD)
            dk += dot(probs[1, j, rows], q[:, cols], NN)
            dv += dot(probs[0, j, rows], g[:, cols], NN)
        return dk * inv_scale, dv

    holder = (xc < 3) | (xc == 6)
    held_slot = jnp.where(xc == 6, 3, xc)
    held_rows = pl.ds(pl.multiple_of(held_slot * piece, piece), piece)

    def rx_copy(slot):
        return remote(
            prompt_bf.at[:, slot * piece : (slot + 1) * piece, :], part_x.at[xc],
            rx_send.at[slot], rx_recv.at[xc], y * ROW + HOLDERS[slot], head,
        )

    def rx_got(slot):
        return remote(part_x.at[slot], part_x.at[slot], rx_send.at[0], rx_recv.at[slot], leaf, head)

    dk, dv = grad_of(0, 0, BLK)
    prompt_grad[0], prompt_grad[1] = dk, dv
    prompt_bf[0], prompt_bf[1] = dk.astype(jnp.bfloat16), dv.astype(jnp.bfloat16)
    for slot in range(chips):
        pl.when(xc != HOLDERS[slot])(lambda slot=slot: rx_copy(slot).start())
        pending.append(lambda slot=slot: pl.when(xc != HOLDERS[slot])(lambda: rx_copy(slot).wait_send()))

    def grad_copy(slot, to):
        return remote(grads.at[slot], near.at[slot], grad_send.at[slot], grad_recv.at[slot], to, head)

    dk, dv = grad_of(side + 1, own0 - side * tok, tok)
    grads[0, 0], grads[0, 1] = dk.astype(jnp.bfloat16), dv.astype(jnp.bfloat16)
    pl.when(leaf >= 2)(lambda: grad_copy(0, sibling).start())
    pending.append(lambda: pl.when(leaf >= 2)(lambda: grad_copy(0, sibling).wait_send()))

    rest = REACH - side
    dk, dv = grad_of(rest + 1, own0 - rest * tok, tok)
    grads[2, 0], grads[2, 1] = dk.astype(jnp.bfloat16), dv.astype(jnp.bfloat16)
    pl.when(leaf >= rest)(lambda: grad_copy(2, leaf - rest).start())
    pending.append(lambda: pl.when(leaf >= rest)(lambda: grad_copy(2, leaf - rest).wait_send()))

    own_grad[0], own_grad[1] = grad_of(3, own0 - 2 * tok, tok)

    @pl.when(leaf >= 2)
    def _():
        grad_copy(0, sibling).wait_recv()
        grads[1] = (own_grad[...] + near[0].astype(jnp.float32)).astype(jnp.bfloat16)
        grad_copy(1, leaf - 2).start()

    pending.append(lambda: pl.when(leaf >= 2)(lambda: grad_copy(1, leaf - 2).wait_send()))

    def rr_copy():
        return remote(sum_x, part_root.at[y * chips + held_slot], rr_send, rr_recv, 0, head)

    @pl.when(holder)
    def _():
        sum_all = prompt_grad[:, held_rows, :]
        for off in range(1, ROW):
            slot = lax.rem(xc + off, ROW)
            rx_got(slot).wait_recv()
            sum_all += part_x[slot].astype(jnp.float32)
        sum_x[...] = sum_all.astype(jnp.bfloat16)
        pl.when(leaf > 0)(lambda: rr_copy().start())

    pending.append(lambda: pl.when(holder & (leaf > 0))(lambda: rr_copy().wait_send()))

    own_grad[0], own_grad[1] = grad_of(1, own0, tok)

    win_t[0] = win[0].T
    win_t[1] = win[1].T
    for j in range(heads_here):
        cols = slice(j * HD, (j + 1) * HD)
        attn[:, cols] = dot(win_t[1], probs[0, j], NN).T.astype(jnp.bfloat16)
    out_copy = pltpu.make_async_copy(attn, attn_out, store_sem.at[0])
    out_copy.start()
    pending.append(out_copy.wait)
    for j in range(heads_here):
        cols = slice(j * HD, (j + 1) * HD)
        dq[:, cols] = (dot(win_t[0], probs[1, j], NN).T * inv_scale).astype(jnp.bfloat16)
    dq_copy = pltpu.make_async_copy(dq, query_grad, store_sem.at[1])
    dq_copy.start()
    pending.append(dq_copy.wait)

    for wait in pending:
        wait()

    for slot, off in ((1, 2), (2, side)):
        @pl.when(leaf + off < leaves)
        def _():
            grad_copy(slot, leaf).wait_recv()
            own_grad[...] += near[slot].astype(jnp.float32)

    @pl.when(leaf == 0)
    def _():
        others = part_root.at[pl.ds(1, rows_y * chips - 1)]
        remote(others, others, rr_send, rr_recv, leaf, head).wait_recv()
        part_root[0] = sum_x[...]
        for slot in range(chips):
            rows = slice(slot * piece, (slot + 1) * piece)
            total = own_grad[:, rows, :]
            for row in range(rows_y):
                total += part_root[row * chips + slot].astype(jnp.float32)
            own_grad[:, rows, :] = total

    key_grad[...] = own_grad[0].astype(jnp.bfloat16)
    value_grad[...] = own_grad[1].astype(jnp.bfloat16)


def store(*refs):
    copies = [pltpu.make_async_copy(refs[i], refs[4 + i], refs[8].at[i]) for i in range(4)]
    for copy in copies:
        copy.start()
    for copy in copies:
        copy.wait()


def on_device(leaves, groups, queries, key_rows, value_rows, out_grad, ancestry, block_fill):
    tok, width = queries.shape
    heads_here = width // HD
    wide = BLK + REACH * tok
    chips = ROW // 2
    piece = BLK // chips
    bf16, f32 = jnp.bfloat16, jnp.float32
    anywhere = pl.BlockSpec(memory_space=pl.ANY)
    in_hbm = pl.BlockSpec(memory_space=pltpu.HBM)
    in_vmem = pl.BlockSpec(memory_space=pltpu.VMEM)
    dma = pltpu.SemaphoreType.DMA
    held = pl.pallas_call(
        functools.partial(kernel, leaves, groups),
        out_shape=(
            pltpu.VMEM((tok, width), bf16),
            pltpu.VMEM((tok, width), bf16),
            pltpu.VMEM((tok, HD), bf16),
            pltpu.VMEM((tok, HD), bf16),
        ),
        in_specs=[in_hbm] * 6,
        out_specs=(anywhere, anywhere, in_vmem, in_vmem),
        scratch_shapes=[
            pltpu.VMEM((tok, width), bf16),
            pltpu.VMEM((tok, width), bf16),
            pltpu.VMEM((2,) + key_rows.shape, bf16),
            pltpu.VMEM((2, wide, HD), bf16),
            pltpu.VMEM((2, HD, wide), bf16),
            pltpu.VMEM((wide, tok), f32),
            pltpu.VMEM((heads_here, wide, tok), f32),
            pltpu.VMEM((heads_here, wide, tok), f32),
            pltpu.VMEM((REACH + 1, heads_here, 8, tok), f32),
            pltpu.VMEM((2, heads_here, wide, tok), bf16),
            pltpu.VMEM((tok, width), bf16),
            pltpu.VMEM((tok, width), bf16),
            pltpu.VMEM((REACH, 2, tok, HD), bf16),
            pltpu.VMEM((2, tok, HD), f32),
            pltpu.VMEM((2, BLK, HD), f32),
            pltpu.VMEM((2, BLK, HD), bf16),
            pltpu.VMEM((REACH, 2, tok, HD), bf16),
            pltpu.VMEM((ROW, 2, piece, HD), bf16),
            pltpu.VMEM((2, piece, HD), bf16),
            pltpu.VMEM((leaves // 2, 2, piece, HD), bf16),
            pltpu.SMEM((8, ancestry.shape[1]), jnp.int32),
            pltpu.SMEM(block_fill.shape, jnp.int32),
            dma((6,)),
            dma((2,)),
            dma((groups,)),
            dma((groups,)),
            dma((REACH, max(1, groups // 2))),
            dma((REACH, max(1, groups // 2))),
            dma((leaves,)),
            dma,
            dma((ROW,)),
            dma((ROW,)),
            dma((REACH,)),
            dma((REACH,)),
            dma((ROW,)),
            dma((ROW,)),
            dma,
            dma,
            pltpu.SemaphoreType.REGULAR,
            pltpu.SemaphoreType.REGULAR,
        ],
        compiler_params=pltpu.CompilerParams(
            collective_id=0, has_side_effects=True, vmem_limit_bytes=50 * 2**20
        ),
    )(
        *(
            pltpu.with_memory_space_constraint(a, pltpu.HBM)
            for a in (queries, key_rows, value_rows, out_grad, ancestry, block_fill)
        )
    )
    return pl.pallas_call(
        store,
        out_shape=[jax.ShapeDtypeStruct(a.shape, a.dtype) for a in held],
        in_specs=[anywhere] * 4,
        out_specs=[in_hbm] * 4,
        scratch_shapes=[dma((4,))],
    )(*(pltpu.with_memory_space_constraint(a, pltpu.VMEM) for a in held))


def solution(mesh):
    placed = (
        P("leaf", "head"),
        P(("leaf", "head"), None),
        P(("leaf", "head"), None),
        P("leaf", "head"),
        P(),
        P(),
    )
    return jax.shard_map(
        functools.partial(on_device, mesh.shape["leaf"], mesh.shape["head"]),
        mesh=mesh,
        in_specs=placed,
        out_specs=(P("leaf", "head"), P("leaf", "head"), P("leaf", "head"), P("leaf", "head")),
        check_vma=False,
    )
```

```python
import functools
import math

import jax
import jax.numpy as jnp
from jax import lax
from jax.experimental import pallas as pl
from jax.experimental.pallas import tpu as pltpu
from jax.sharding import PartitionSpec as P

HD = 128
BLK = 128
REACH = 4
ROW = 8
HOLDERS = (0, 1, 2, 6)
MESH = pl.DeviceIdType.MESH
NEG = -1e30
NT = (((1,), (1,)), ((), ()))
NN = (((1,), (0,)), ((), ()))
dot = functools.partial(lax.dot_general, preferred_element_type=jnp.float32)


def kernel(
    leaves, groups, queries, key_rows, value_rows, out_grad, ancestry, fills,
    attn_out, query_grad, key_grad, value_grad,
    q, g, kv_in, win, win_t, bias, scores, d_weights, stats, probs, attn, dq,
    grads, own_grad, prompt_grad, prompt_bf, near, part_x, sum_x, part_root,
    anc, block_fill,
    load_sem, store_sem, a2a_send, a2a_recv, shift_send, shift_recv, root_send, root_recv,
    gather_send, gather_recv, grad_send, grad_recv, rx_send, rx_recv, rr_send, rr_recv, ready, zready,
):
    leaf = lax.axis_index("leaf")
    head = lax.axis_index("head")
    tok = q.shape[0]
    heads_here = q.shape[1] // HD
    rows_in = kv_in.shape[1]
    rows_y = leaves // ROW
    chips = ROW // 2
    piece = BLK // chips
    wide = win.shape[1]
    own0 = wide - tok
    y = leaf // ROW
    xc = leaf % ROW
    x = xc // 2
    core = leaf % 2
    sibling = leaf + 1 - 2 * core
    half = groups // 2
    lower = head < half
    inv_scale = 1.0 / math.sqrt(HD)
    log_scale = inv_scale * math.log2(math.e)

    base = pl.multiple_of((2 * leaf) // 8 * 8, 8)
    loads = [
        pltpu.make_async_copy(key_rows, kv_in.at[0], load_sem.at[0]),
        pltpu.make_async_copy(value_rows, kv_in.at[1], load_sem.at[1]),
        pltpu.make_async_copy(queries, q, load_sem.at[2]),
        pltpu.make_async_copy(out_grad, g, load_sem.at[3]),
        pltpu.make_async_copy(ancestry.at[pl.ds(base, 8)], anc, load_sem.at[4]),
        pltpu.make_async_copy(fills, block_fill, load_sem.at[5]),
    ]
    for load in loads[:2]:
        load.start()

    pending = []
    barrier = pltpu.get_barrier_semaphore()

    def greet(leaf_to, head_to):
        pl.semaphore_signal(barrier, inc=1, device_id=(leaf_to, head_to), device_id_type=MESH)

    for off in range(1, groups):
        to = lax.rem(head + off, groups)
        pl.when(lower | (to >= half))(functools.partial(greet, leaf, to))
    for off in range(1, ROW):
        greet(y * ROW + lax.rem(xc + off, ROW), head)
    for off in range(1, REACH):
        pl.when(leaf >= off)(functools.partial(greet, leaf - off, head))
        pl.when(leaf + off < leaves)(functools.partial(greet, leaf + off, head))

    @pl.when(leaf == 0)
    def _():
        @pl.loop(1, leaves)
        def _(to):
            greet(to, head)

    for load in loads[:2]:
        load.wait()
    greeted = jnp.where(lower, half, groups) - 1 + ROW - 1 + jnp.minimum(leaf, REACH - 1) + jnp.minimum(leaves - 1 - leaf, REACH - 1)
    greeted += jnp.where(leaf == 0, 0, 1)
    pl.semaphore_wait(barrier, greeted)

    @pl.when((leaf > 0) & (core == 0))
    def _():
        pl.semaphore_signal(ready, inc=1, device_id=(0, head), device_id_type=MESH)

    @pl.when(head >= half)
    def _():
        for to in range(half):
            pl.semaphore_signal(zready, inc=1, device_id=(leaf, to), device_id_type=MESH)

    def remote(src, dst, send, recv, leaf_to, head_to):
        return pltpu.make_async_remote_copy(
            src_ref=src, dst_ref=dst, send_sem=send, recv_sem=recv,
            device_id=(leaf_to, head_to), device_id_type=MESH,
        )

    def a2a_copy(off):
        to = lax.rem(head + off, groups)
        return remote(
            kv_in.at[:, :, pl.ds(pl.multiple_of(to * HD, HD), HD)],
            win.at[:, pl.ds(pl.multiple_of(own0 + head * rows_in, 32), rows_in), :],
            a2a_send.at[off], a2a_recv.at[off], leaf, to,
        )

    for off in range(1, groups):
        to = lax.rem(head + off, groups)
        pl.when((head >= half) | (to < half))(lambda off=off: a2a_copy(off).start())
        pending.append(a2a_copy(off).wait_send)
    for load in loads[2:]:
        load.start()
    win[:, pl.ds(pl.multiple_of(own0 + head * rows_in, 32), rows_in), :] = kv_in[
        :, :, pl.ds(pl.multiple_of(head * HD, HD), HD)
    ]
    for off in range(1, REACH):
        rows = pl.ds(own0 - off * tok, tok)

        @pl.when(leaf < off)
        def _():
            win[:, rows, :] = jnp.zeros((2, tok, HD), win.dtype)

    loads[4].wait()
    loads[5].wait()
    key_iota = lax.broadcasted_iota(jnp.int32, (BLK, BLK), 0)
    query_iota = lax.broadcasted_iota(jnp.int32, (BLK, BLK), 1)
    blocks_dev = tok // BLK
    for col in range(wide // BLK):
        block = 0 if col == 0 else (leaf - (REACH - 1)) * blocks_dev + col - 1
        at = 0 if col == 0 else jnp.maximum(block, 0)
        fill = block_fill[at]
        for row in range(blocks_dev):
            link = anc[2 * leaf - base + row, at]
            if col > 0:
                link = jnp.where(block >= 1, link, 0)
            limit = jnp.where(link == 1, fill, 0)
            allowed = (key_iota < limit) & (
                key_iota + block * BLK <= query_iota + (leaf * blocks_dev + row) * BLK
            )
            bias[col * BLK : (col + 1) * BLK, row * BLK : (row + 1) * BLK] = jnp.where(allowed, 0.0, NEG)

    side = jnp.where(core == 0, 1, REACH - 1)

    parts = max(1, groups // 2)
    part_rows = tok // parts

    def part_of(off, part):
        return win.at[:, pl.ds(pl.multiple_of(own0 - off * tok + part * part_rows, 32), part_rows), :]

    def shift_copy(off, part):
        return remote(
            part_of(0, part), part_of(off, part),
            shift_send.at[off, part], shift_recv.at[off, part], leaf + off, head,
        )

    def swap_copy(part):
        lands = REACH - side
        return remote(
            part_of(2, part), part_of(lands, part),
            shift_send.at[0, part], shift_recv.at[lands, part], sibling, head,
        )

    def root_copy(to):
        at = to % ROW // 2 * piece
        return remote(
            win.at[:, pl.ds(pl.multiple_of(own0 + at, piece), piece), :],
            win.at[:, pl.ds(pl.multiple_of(at, piece), piece), :],
            root_send.at[to], root_recv, to, head,
        )

    def scatter():
        pl.semaphore_wait(ready, rows_y * chips - 1)
        for row in sorted(range(rows_y), key=lambda r: -min(r, rows_y - r)):
            @pl.loop(int(row == 0), chips)
            def _(i):
                root_copy(row * ROW + 2 * i).start()

        win[:, :piece, :] = win[:, own0 : own0 + piece, :]

    def send_upper():
        pl.semaphore_wait(zready, groups - half)
        for to in range(half, groups):
            a2a_copy(to - head).start()

    per_part = groups // parts
    for part in range(parts):
        for source in range(part * per_part, (part + 1) * per_part):
            off = lax.rem(head - source + groups, groups)
            pl.when(off > 0)(lambda off=off: a2a_copy(off).wait_recv())
        for off in (2, side):
            pl.when(leaf + off < leaves)(lambda off=off: shift_copy(off, part).start())
        if part * part_rows < BLK <= (part + 1) * part_rows:
            pl.when(leaf == 0)(scatter)
            pl.when(lower)(send_upper)

    def shift_done():
        for part in range(parts):
            for off in (2, side):
                pl.when(leaf + off < leaves)(lambda off=off: shift_copy(off, part).wait_send())

    pending.append(shift_done)

    def root_done():
        @pl.when(leaf == 0)
        def _():
            @pl.loop(1, rows_y * chips)
            def _(i):
                root_copy(2 * i).wait_send()

    pending.append(root_done)

    loads[2].wait()
    loads[3].wait()

    def meet(first):
        slot, rows = first // BLK, slice(first, first + BLK)
        keys, values, added = win[0, rows], win[1, rows], bias[rows]
        for j in range(heads_here):
            cols = slice(j * HD, (j + 1) * HD)
            part = dot(keys, q[:, cols], NT) + added
            top = part.reshape(BLK // 8, 8, tok).max(0).max(0, keepdims=True) * log_scale
            d = dot(values, g[:, cols], NT)
            d_weights[j, rows] = d
            e = jnp.exp2(part * log_scale - top)
            scores[j, rows] = e
            stats[slot, j, 0:1] = top
            stats[slot, j, 1:2] = e.reshape(BLK // 8, 8, tok).sum(0).sum(0, keepdims=True)
            stats[slot, j, 2:3] = (e * d).reshape(BLK // 8, 8, tok).sum(0).sum(0, keepdims=True)

    for first in range(own0, wide, BLK):
        meet(first)

    my_piece = pl.ds(pl.multiple_of(x * piece, piece), piece)

    def gather_copy(off):
        return remote(
            win.at[:, my_piece, :], win.at[:, my_piece, :],
            gather_send.at[off], gather_recv.at[x], y * ROW + lax.rem(xc + off, ROW), head,
        )

    def gather_got(slot):
        rows = win.at[:, slot * piece : (slot + 1) * piece, :]
        return remote(rows, rows, gather_send.at[0], gather_recv.at[slot], leaf, head)

    @pl.when(core == 0)
    def _():
        pl.when(leaf > 0)(lambda: root_copy(leaf).wait_recv())
        for off in range(1, ROW):
            gather_copy(off).start()

    def gather_done():
        for off in range(1, ROW):
            gather_copy(off).wait_send()

    pending.append(lambda: pl.when(core == 0)(gather_done))

    early, late = range(max(1, parts // 2)), range(max(1, parts // 2), parts)

    def swap(some):
        for part in some:
            shift_copy(2, part).wait_recv()
            swap_copy(part).start()

    def arrive(off, some):
        for part in some:
            shift_copy(off, part).wait_recv()

    def swap_done():
        for part in range(parts):
            swap_copy(part).wait_send()

    pending.append(lambda: pl.when(leaf >= 2)(swap_done))
    pl.when(leaf >= 2)(functools.partial(swap, early))
    meet(own0 - 2 * tok)
    pl.when(leaf >= 2)(functools.partial(swap, late))
    for off in (1, 3):
        pl.when(leaf >= off)(functools.partial(arrive, off, early))
        meet(own0 - off * tok)
    meet(own0 - 2 * tok + BLK)
    for off in (1, 3):
        pl.when(leaf >= off)(functools.partial(arrive, off, late))
        meet(own0 - off * tok + BLK)
    for slot in range(chips):
        pl.when((core == 1) | (x != slot))(lambda slot=slot: gather_got(slot).wait_recv())
    meet(0)

    slots = wide // BLK
    for j in range(heads_here):
        tops = [stats[slot, j, 0:1] for slot in range(slots)]
        top = functools.reduce(jnp.maximum, tops)
        scales = [jnp.exp2(t - top) for t in tops]
        inverse = 1.0 / sum(stats[slot, j, 1:2] * scales[slot] for slot in range(slots))
        stats[0, j, 4:5] = inverse * sum(stats[slot, j, 2:3] * scales[slot] for slot in range(slots))
        for slot in range(slots):
            stats[slot, j, 3:4] = inverse * scales[slot]

    def grad_of(first, count):
        for j in range(heads_here):
            delta = stats[0, j, 4:5]
            for r in range(0, count, BLK):
                factor = stats[(first + r) // BLK, j, 3:4]
                some = pl.ds(pl.multiple_of(first + r, BLK), BLK)
                w = scores[j, some] * factor
                probs[0, j, some] = w.astype(jnp.bfloat16)
                probs[1, j, some] = (w * (d_weights[j, some] - delta)).astype(jnp.bfloat16)
        rows = pl.ds(pl.multiple_of(first, BLK), count)
        dk = jnp.zeros((count, HD), jnp.float32)
        dv = jnp.zeros((count, HD), jnp.float32)
        for j in range(heads_here):
            cols = slice(j * HD, (j + 1) * HD)
            dk += dot(probs[1, j, rows], q[:, cols], NN)
            dv += dot(probs[0, j, rows], g[:, cols], NN)
        return dk * inv_scale, dv

    holder = (xc < 3) | (xc == 6)
    held_slot = jnp.where(xc == 6, 3, xc)
    held_rows = pl.ds(pl.multiple_of(held_slot * piece, piece), piece)

    def rx_copy(slot):
        return remote(
            prompt_bf.at[:, slot * piece : (slot + 1) * piece, :], part_x.at[xc],
            rx_send.at[slot], rx_recv.at[xc], y * ROW + HOLDERS[slot], head,
        )

    def rx_got(slot):
        return remote(part_x.at[slot], part_x.at[slot], rx_send.at[0], rx_recv.at[slot], leaf, head)

    dk, dv = grad_of(0, BLK)
    prompt_grad[0], prompt_grad[1] = dk, dv
    prompt_bf[0], prompt_bf[1] = dk.astype(jnp.bfloat16), dv.astype(jnp.bfloat16)
    for slot in range(chips):
        pl.when(xc != HOLDERS[slot])(lambda slot=slot: rx_copy(slot).start())
        pending.append(lambda slot=slot: pl.when(xc != HOLDERS[slot])(lambda: rx_copy(slot).wait_send()))

    def grad_copy(slot, to):
        return remote(grads.at[slot], near.at[slot], grad_send.at[slot], grad_recv.at[slot], to, head)

    dk, dv = grad_of(own0 - side * tok, tok)
    grads[0, 0], grads[0, 1] = dk.astype(jnp.bfloat16), dv.astype(jnp.bfloat16)
    pl.when(leaf >= 2)(lambda: grad_copy(0, sibling).start())
    pending.append(lambda: pl.when(leaf >= 2)(lambda: grad_copy(0, sibling).wait_send()))

    rest = REACH - side
    dk, dv = grad_of(own0 - rest * tok, tok)
    grads[2, 0], grads[2, 1] = dk.astype(jnp.bfloat16), dv.astype(jnp.bfloat16)
    pl.when(leaf >= rest)(lambda: grad_copy(2, leaf - rest).start())
    pending.append(lambda: pl.when(leaf >= rest)(lambda: grad_copy(2, leaf - rest).wait_send()))

    own_grad[0], own_grad[1] = grad_of(own0 - 2 * tok, tok)

    @pl.when(leaf >= 2)
    def _():
        grad_copy(0, sibling).wait_recv()
        grads[1] = (own_grad[...] + near[0].astype(jnp.float32)).astype(jnp.bfloat16)
        grad_copy(1, leaf - 2).start()

    pending.append(lambda: pl.when(leaf >= 2)(lambda: grad_copy(1, leaf - 2).wait_send()))

    def rr_copy():
        return remote(sum_x, part_root.at[y * chips + held_slot], rr_send, rr_recv, 0, head)

    @pl.when(holder)
    def _():
        sum_all = prompt_grad[:, held_rows, :]
        for off in range(1, ROW):
            slot = lax.rem(xc + off, ROW)
            rx_got(slot).wait_recv()
            sum_all += part_x[slot].astype(jnp.float32)
        sum_x[...] = sum_all.astype(jnp.bfloat16)
        pl.when(leaf > 0)(lambda: rr_copy().start())

    pending.append(lambda: pl.when(holder & (leaf > 0))(lambda: rr_copy().wait_send()))

    own_grad[0], own_grad[1] = grad_of(own0, tok)

    win_t[0] = win[0].T
    win_t[1] = win[1].T
    for j in range(heads_here):
        cols = slice(j * HD, (j + 1) * HD)
        attn[:, cols] = dot(win_t[1], probs[0, j], NN).T.astype(jnp.bfloat16)
    out_copy = pltpu.make_async_copy(attn, attn_out, store_sem.at[0])
    out_copy.start()
    pending.append(out_copy.wait)
    for j in range(heads_here):
        cols = slice(j * HD, (j + 1) * HD)
        dq[:, cols] = (dot(win_t[0], probs[1, j], NN).T * inv_scale).astype(jnp.bfloat16)
    dq_copy = pltpu.make_async_copy(dq, query_grad, store_sem.at[1])
    dq_copy.start()
    pending.append(dq_copy.wait)

    for wait in pending:
        wait()

    for slot, off in ((1, 2), (2, side)):
        @pl.when(leaf + off < leaves)
        def _():
            grad_copy(slot, leaf).wait_recv()
            own_grad[...] += near[slot].astype(jnp.float32)

    @pl.when(leaf == 0)
    def _():
        others = part_root.at[pl.ds(1, rows_y * chips - 1)]
        remote(others, others, rr_send, rr_recv, leaf, head).wait_recv()
        part_root[0] = sum_x[...]
        for slot in range(chips):
            rows = slice(slot * piece, (slot + 1) * piece)
            total = own_grad[:, rows, :]
            for row in range(rows_y):
                total += part_root[row * chips + slot].astype(jnp.float32)
            own_grad[:, rows, :] = total

    key_grad[...] = own_grad[0].astype(jnp.bfloat16)
    value_grad[...] = own_grad[1].astype(jnp.bfloat16)


def store(*refs):
    copies = [pltpu.make_async_copy(refs[i], refs[4 + i], refs[8].at[i]) for i in range(4)]
    for copy in copies:
        copy.start()
    for copy in copies:
        copy.wait()


def on_device(leaves, groups, queries, key_rows, value_rows, out_grad, ancestry, block_fill):
    tok, width = queries.shape
    heads_here = width // HD
    wide = BLK + REACH * tok
    chips = ROW // 2
    piece = BLK // chips
    bf16, f32 = jnp.bfloat16, jnp.float32
    anywhere = pl.BlockSpec(memory_space=pl.ANY)
    in_hbm = pl.BlockSpec(memory_space=pltpu.HBM)
    in_vmem = pl.BlockSpec(memory_space=pltpu.VMEM)
    dma = pltpu.SemaphoreType.DMA
    held = pl.pallas_call(
        functools.partial(kernel, leaves, groups),
        out_shape=(
            pltpu.VMEM((tok, width), bf16),
            pltpu.VMEM((tok, width), bf16),
            pltpu.VMEM((tok, HD), bf16),
            pltpu.VMEM((tok, HD), bf16),
        ),
        in_specs=[in_hbm] * 6,
        out_specs=(anywhere, anywhere, in_vmem, in_vmem),
        scratch_shapes=[
            pltpu.VMEM((tok, width), bf16),
            pltpu.VMEM((tok, width), bf16),
            pltpu.VMEM((2,) + key_rows.shape, bf16),
            pltpu.VMEM((2, wide, HD), bf16),
            pltpu.VMEM((2, HD, wide), bf16),
            pltpu.VMEM((wide, tok), f32),
            pltpu.VMEM((heads_here, wide, tok), f32),
            pltpu.VMEM((heads_here, wide, tok), f32),
            pltpu.VMEM((wide // BLK, heads_here, 8, tok), f32),
            pltpu.VMEM((2, heads_here, wide, tok), bf16),
            pltpu.VMEM((tok, width), bf16),
            pltpu.VMEM((tok, width), bf16),
            pltpu.VMEM((REACH, 2, tok, HD), bf16),
            pltpu.VMEM((2, tok, HD), f32),
            pltpu.VMEM((2, BLK, HD), f32),
            pltpu.VMEM((2, BLK, HD), bf16),
            pltpu.VMEM((REACH, 2, tok, HD), bf16),
            pltpu.VMEM((ROW, 2, piece, HD), bf16),
            pltpu.VMEM((2, piece, HD), bf16),
            pltpu.VMEM((leaves // 2, 2, piece, HD), bf16),
            pltpu.SMEM((8, ancestry.shape[1]), jnp.int32),
            pltpu.SMEM(block_fill.shape, jnp.int32),
            dma((6,)),
            dma((2,)),
            dma((groups,)),
            dma((groups,)),
            dma((REACH, max(1, groups // 2))),
            dma((REACH, max(1, groups // 2))),
            dma((leaves,)),
            dma,
            dma((ROW,)),
            dma((ROW,)),
            dma((REACH,)),
            dma((REACH,)),
            dma((ROW,)),
            dma((ROW,)),
            dma,
            dma,
            pltpu.SemaphoreType.REGULAR,
            pltpu.SemaphoreType.REGULAR,
        ],
        compiler_params=pltpu.CompilerParams(
            collective_id=0, has_side_effects=True, vmem_limit_bytes=50 * 2**20
        ),
    )(
        *(
            pltpu.with_memory_space_constraint(a, pltpu.HBM)
            for a in (queries, key_rows, value_rows, out_grad, ancestry, block_fill)
        )
    )
    return pl.pallas_call(
        store,
        out_shape=[jax.ShapeDtypeStruct(a.shape, a.dtype) for a in held],
        in_specs=[anywhere] * 4,
        out_specs=[in_hbm] * 4,
        scratch_shapes=[dma((4,))],
    )(*(pltpu.with_memory_space_constraint(a, pltpu.VMEM) for a in held))


def solution(mesh):
    placed = (
        P("leaf", "head"),
        P(("leaf", "head"), None),
        P(("leaf", "head"), None),
        P("leaf", "head"),
        P(),
        P(),
    )
    return jax.shard_map(
        functools.partial(on_device, mesh.shape["leaf"], mesh.shape["head"]),
        mesh=mesh,
        in_specs=placed,
        out_specs=(P("leaf", "head"), P("leaf", "head"), P("leaf", "head"), P("leaf", "head")),
        check_vma=False,
    )
```
